32 devices in a mesh: dp: 16 (over z, y, core), mp: 2 (over x).
Axes of the slice: x: 2, y: 2, z: 4, core: 2. Of those that a mesh axis runs over, the one named last changes fastest.
Arguments:
- residual: bfloat16 [4096, 4608], P('dp', 'mp'), may hold values from -6 to 6
- out_grad: bfloat16 [4096, 4608], P('dp', 'mp'), may hold values from -6 to 6
- ffn_weights: bfloat16 [3, 64, 4608], P(None, 'mp'), may hold values from -0.09375 to 0.09375
- norm_gain: float32 [4608], replicated, may hold values from 0.1 to 1.9
- exponents: int32 [3], replicated, may hold values from 3 to 6, as said below
- sign_bits: int32 [4608], replicated, may hold values from 0 to 1
Outputs:
- resid_grad: bfloat16 [4096, 4608], P('dp', 'mp')
- weight_grads: bfloat16 [3, 64, 4608], P(None, 'mp')
The draws below stay inside these ranges and needn't reach their ends.
Inputs may be any that keep to these rules, and one draw needn't show every extreme that they name: `exponents`: one exponent for each of the gate, up and down gradients; every draw holds both 3 and 6. `sign_bits`: one bit per feature.
All inputs are finite; a program needn't handle non-finite values.
Results may differ from the reference program's by a relative error of at most 0.01.
Values may be sent and summed in bfloat16 or wider, within the bound.
A program may use at most 64 MiB of HBM per device.

```python
import math
import jax
import jax.numpy as jnp
from jax import lax

D = 4608
TOK_DEV = 256
BUCKET_DEV = 32
TOKENS = 4096
BUCKET = 64
N_DP = 16
N_MP = 2


def draw_exponents(key, part):
    key = jax.random.fold_in(key, 11)
    third = jax.random.randint(jax.random.fold_in(key, 1), (1,), 3, 7, dtype=jnp.int32)
    values = jnp.concatenate([jnp.array([3, 6], dtype=jnp.int32), third])
    order = jax.random.permutation(jax.random.fold_in(key, 2), jnp.arange(3, dtype=jnp.int32))
    return values[order].astype(jnp.int32)


def place_ends(drawn, rng, smallest, largest):
    longest = drawn.shape.index(max(drawn.shape))
    spots = []
    for shift in (0, 1):
        where = [jax.random.randint(jax.random.fold_in(rng, axis), (), 0, length) for axis, length in enumerate(drawn.shape)]
        where[longest] = (where[longest] + shift) % drawn.shape[longest]
        spots.append(tuple(where))
    return drawn.at[spots[0]].set(smallest).at[spots[1]].set(largest)


def block_scale(key, extent, cuts, least, high):
    def one(axis_at, blocks):
        steps = jax.random.uniform(jax.random.fold_in(jax.random.fold_in(key, 6), axis_at), (blocks,), jnp.float32, least / len(cuts), high / len(cuts))
        return jnp.repeat(jnp.exp(steps), extent[axis_at] // blocks).reshape((-1,) + (1,) * (len(extent) - axis_at - 1))

    level = one(*cuts[0])
    for cut in cuts[1:]:
        level = level * one(*cut)
    return level


def scatter_about(own_key, shape, width, limit, split=(), kind=jnp.bfloat16):
    values = width * jax.random.normal(own_key, shape, jnp.float32)
    if split:
        values = values * block_scale(own_key, shape, split, -0.22, 0.18)
    return jnp.clip(values, -limit, limit).astype(kind)


def setup_inputs(seed: int = 0) -> dict:
    key_list = jax.random.split(jax.random.key(seed), 7)
    residual = scatter_about(key_list[0], (TOKENS, D), 1.0, 6.0, ((0, 16), (1, 2)))
    out_grad = scatter_about(key_list[1], (TOKENS, D), 1.0, 6.0, ((0, 16), (1, 2)))
    ffn_weights = scatter_about(key_list[2], (3, BUCKET, D), D ** -0.5, 0.09375, ((1, 2),))
    norm_gain = jnp.clip(1.0 + 0.18 * jax.random.normal(key_list[3], (D,), jnp.float32), 0.1, 1.9)
    exponents = draw_exponents(jax.random.fold_in(key_list[6], 71), 0)
    sign_bits = place_ends(jax.random.randint(key_list[5], (D,), 0, 2), jax.random.fold_in(key_list[5], 1), 0, 1).astype(jnp.int32)
    return dict(residual=residual, out_grad=out_grad, ffn_weights=ffn_weights, norm_gain=norm_gain, exponents=exponents, sign_bits=sign_bits)


def hadamard():
    indices = jnp.arange(128, dtype=jnp.int32)
    anded = jnp.bitwise_and(indices[:, None], indices[None, :])
    parity = jnp.zeros((128, 128), jnp.int32)
    for offset in range(7):
        parity = parity + jnp.bitwise_and(jnp.right_shift(anded, offset), 1)
    return (1 - 2 * (parity % 2)).astype(jnp.float32) / math.sqrt(128.0)

def gelu_parts(values):
    tanh_input = 0.7978845608 * (values + 0.044715 * values * values * values)
    tanhed = jnp.tanh(tanh_input)
    forward = 0.5 * values * (1.0 + tanhed)
    gelu_slope = 0.5 * (1.0 + tanhed) + 0.5 * values * (1.0 - tanhed * tanhed) * 0.7978845608 * (1.0 + 3.0 * 0.044715 * values * values)
    return (forward, gelu_slope)

def reference(residual, out_grad, ffn_weights, norm_gain, exponents, sign_bits):
    hadamard_table = hadamard()
    sign_table = (2 * sign_bits - 1).astype(jnp.float32).reshape(D // 128, 128)
    scales = jnp.exp2(exponents.astype(jnp.float32))
    grouped = ffn_weights.astype(jnp.float32).reshape(3, N_MP, BUCKET_DEV, D)

    def one_group(running, pieces):
        full_rows, grads_in = pieces
        rows_wide = full_rows.astype(jnp.float32)
        inverse = lax.rsqrt(lax.optimization_barrier(jnp.mean(rows_wide * rows_wide, axis=1, keepdims=True)) + 1e-06)
        unit_rows = rows_wide * inverse
        normed = (unit_rows * norm_gain).astype(jnp.bfloat16)
        gate_pre = jnp.dot(normed, ffn_weights[0].T, preferred_element_type=jnp.float32)
        up_proj = jnp.dot(normed, ffn_weights[1].T, preferred_element_type=jnp.float32)
        activated, gelu_slope = gelu_parts(gate_pre)
        hidden = (activated * up_proj).astype(jnp.bfloat16)
        hidden_grad = jnp.dot(grads_in, ffn_weights[2].T, preferred_element_type=jnp.float32)
        gate_grad = (hidden_grad * up_proj * gelu_slope).astype(jnp.bfloat16)
        up_grad = (hidden_grad * activated).astype(jnp.bfloat16)
        gate_split = gate_grad.astype(jnp.float32).reshape(-1, N_MP, BUCKET_DEV)
        up_split = up_grad.astype(jnp.float32).reshape(-1, N_MP, BUCKET_DEV)
        terms = jnp.einsum('tgh,ghd->gtd', gate_split, grouped[0]) + jnp.einsum('tgh,ghd->gtd', up_split, grouped[1])
        rounded = lax.optimization_barrier(terms.astype(jnp.bfloat16))
        normed_grad = lax.optimization_barrier(jnp.sum(rounded.astype(jnp.float32), axis=0))
        feature_grad = normed_grad * norm_gain
        row_mean = lax.optimization_barrier(jnp.mean(feature_grad * unit_rows, axis=1, keepdims=True))
        resid_grad = (grads_in.astype(jnp.float32) + inverse * (feature_grad - unit_rows * row_mean)).astype(jnp.bfloat16)
        gate_wgrad = jnp.dot(gate_grad.T, normed, preferred_element_type=jnp.float32)
        up_wgrad = jnp.dot(up_grad.T, normed, preferred_element_type=jnp.float32)
        down_wgrad = jnp.dot(hidden.T, grads_in, preferred_element_type=jnp.float32)
        stacked = jnp.stack([gate_wgrad, up_wgrad, down_wgrad]).reshape(3, BUCKET, D // 128, 128) * sign_table
        rotated = jnp.einsum('kubj,jc->kubc', stacked, hadamard_table, precision=lax.Precision.HIGHEST)
        quantized = jnp.clip(rotated * scales[:, None, None, None], -127.0, 127.0).astype(jnp.bfloat16)
        quantized = lax.optimization_barrier(quantized)
        return (running + quantized.astype(jnp.float32), resid_grad)
    start_sum = jnp.zeros((3, BUCKET, D // 128, 128), jnp.float32)
    grouped_rows = residual.reshape(N_DP, TOK_DEV, D)
    grouped_grads = out_grad.reshape(N_DP, TOK_DEV, D)
    running, resid_grads = lax.scan(one_group, start_sum, (grouped_rows, grouped_grads))
    summed = lax.optimization_barrier(running.astype(jnp.bfloat16)).astype(jnp.float32)
    factors = jnp.exp2(-exponents.astype(jnp.float32)) / N_DP
    restored = jnp.einsum('kubj,jc->kubc', summed * factors[:, None, None, None], hadamard_table, precision=lax.Precision.HIGHEST) * sign_table
    return (resid_grads.reshape(TOKENS, D), restored.astype(jnp.bfloat16).reshape(3, BUCKET, D))
```

```python
import functools
import math

import jax
import jax.numpy as jnp
from jax import lax
from jax.experimental import pallas as pl
from jax.experimental.pallas import tpu as pltpu
from jax.sharding import PartitionSpec as P

MESH = pl.DeviceIdType.MESH
F32 = jnp.float32
BF16 = jnp.bfloat16


def dot_nt(left, right):
    return lax.dot_general(left, right, (((1,), (1,)), ((), ())), preferred_element_type=F32)


def dot_nn(left, right):
    return lax.dot_general(left, right, (((1,), (0,)), ((), ())), preferred_element_type=F32)


def split_dot(dot, left, right, split_left):
    wide = left if split_left else right
    high = wide.astype(BF16)
    low = (wide - high.astype(F32)).astype(BF16)
    if split_left:
        return dot(high, right) + dot(low, right)
    return dot(left, high) + dot(left, low)


def signs_256():
    rows = lax.broadcasted_iota(jnp.int32, (256, 256), 0)
    cols = lax.broadcasted_iota(jnp.int32, (256, 256), 1)
    anded = jnp.bitwise_and(jnp.bitwise_and(rows, cols), 127)
    for shift in (4, 2, 1):
        anded = jnp.bitwise_xor(anded, jnp.right_shift(anded, shift))
    value = 1 - 2 * jnp.bitwise_and(anded, 1)
    same = jnp.right_shift(rows, 7) == jnp.right_shift(cols, 7)
    return jnp.where(same, value, 0).astype(F32).astype(BF16)


def to_column(row):
    return jnp.broadcast_to(row[0:1], (128, row.shape[1])).T


def pair(ref, first):
    return jnp.concatenate([ref[first], ref[first + 1]], axis=1)


def kernel(
    sizes,
    res_ref,
    og_ref,
    w_ref,
    gain_ref,
    exp_ref,
    sign_ref,
    rg_ref,
    out_ref,
    had,
    normed,
    column,
    wbuf,
    sq_mine,
    sq_peer,
    part,
    part_out,
    part_in,
    terms,
    core_in,
    core_sum,
    y_in,
    y_sum,
    z_in,
    share,
    slots,
    local_sem,
    send_sem,
    recv_sem,
):
    n_dp, blocks, groups, window, starts = sizes
    cols = blocks * 128
    per_block = 3 * groups
    rows_w = 16 * groups
    half = blocks * per_block // 2
    quarter = half // 2
    me = lax.axis_index("dp")
    side = lax.axis_index("mp")
    other = 1 - side
    core = me % 2
    y = (me // 2) % 2
    z = me // 4
    z_near = [z, z + 1 - 2 * (z % 2), (z + 2) % 4, 3 - z]
    first_block = side * blocks
    to_x = (me, other)
    to_core = (me + 1 - 2 * core, side)
    to_y = (me + 2 - 4 * y, side)
    to_z = [None] + [(zz * 4 + y * 2 + core, side) for zz in z_near[1:]]
    count = [0]

    def remote(src, dst, target):
        index = count[0]
        count[0] += 1
        return pltpu.make_async_remote_copy(
            src_ref=src,
            dst_ref=dst,
            send_sem=send_sem.at[index],
            recv_sem=recv_sem.at[index],
            device_id=target,
            device_id_type=MESH,
        )

    started = []

    def send(copy):
        copy.start()
        started.append(copy)

    barrier = pltpu.get_barrier_semaphore()
    partners = [to_x, to_core, to_y] + to_z[1:]
    for target in partners:
        pl.semaphore_signal(barrier, inc=1, device_id=target, device_id_type=MESH)

    own_cols = pl.ds(pl.multiple_of(side * cols, 128), cols)
    peer_cols = pl.ds(pl.multiple_of(other * cols, 128), cols)
    own_w = pltpu.make_async_copy(w_ref.at[:, :, own_cols], wbuf.at[side], local_sem)
    own_w.start()
    wide = res_ref[...].astype(F32)
    ones = jnp.ones((8, cols), BF16)
    sq_mine[...] = split_dot(dot_nt, ones, wide * wide, False)
    had[...] = signs_256()
    pl.semaphore_wait(barrier, len(partners))

    sq_copy = remote(sq_mine, sq_peer, to_x)
    send(sq_copy)
    core_rows = pl.ds(pl.multiple_of(core * (rows_w // 2), 16), rows_w // 2)
    w_copies = {}
    for k in (2, 0, 1):
        w_copies[k] = remote(
            w_ref.at[k, core_rows, peer_cols], wbuf.at[side, k, core_rows], to_x
        )
        send(w_copies[k])

    own_w.wait()
    part[side, 2 * rows_w : 3 * rows_w] = dot_nt(wbuf[side, 2], og_ref[...])
    sq_copy.wait_recv()
    total_sq = sq_mine[...] + sq_peer[...]
    inverse = to_column(lax.rsqrt(total_sq / float(2 * cols) + 1e-06))
    column[0] = inverse
    for j in range(blocks):
        at = slice(128 * j, 128 * j + 128)
        unit = res_ref[:, at].astype(F32) * inverse
        normed[:, at] = (unit * gain_ref[first_block + j]).astype(BF16)
    part[side, : 2 * rows_w] = dot_nt(
        wbuf[side, :2].reshape(2 * rows_w, cols), normed[...]
    )
    part_out[side] = part[side].astype(BF16)
    own_part = remote(part_out.at[side], part_in.at[side], to_x)
    send(own_part)

    shared = {}
    for k in (2, 0, 1):
        w_copies[k].wait_recv()
        shared[k] = remote(
            wbuf.at[other, k, core_rows], wbuf.at[other, k, core_rows], to_core
        )
        send(shared[k])
    shared[2].wait_recv()
    part[other, 2 * rows_w : 3 * rows_w] = dot_nt(wbuf[other, 2], og_ref[...])
    shared[0].wait_recv()
    shared[1].wait_recv()
    part[other, : 2 * rows_w] = dot_nt(
        wbuf[other, :2].reshape(2 * rows_w, cols), normed[...]
    )
    part_out[other] = part[other].astype(BF16)
    peer_part = remote(part_out.at[other], part_in.at[other], to_x)
    send(peer_part)
    own_part.wait_recv()
    peer_part.wait_recv()

    pair_grads = []
    hiddens = []
    row_total = jnp.zeros((1, part.shape[2]), F32)
    for g in range(2):
        full = part[g] + part_in[g].astype(F32)
        gate_pre = full[:rows_w]
        up_proj = full[rows_w : 2 * rows_w]
        hidden_grad = full[2 * rows_w :]
        activated, slope = gelu_parts(gate_pre)
        hiddens.append((activated * up_proj).astype(BF16))
        gate_grad = (hidden_grad * up_proj * slope).astype(BF16)
        up_grad = (hidden_grad * activated).astype(BF16)
        pair_grads += [gate_grad, up_grad]
        row_total = row_total + jnp.sum(
            gate_grad.astype(F32) * gate_pre + up_grad.astype(F32) * up_proj,
            axis=0,
            keepdims=True,
        )
    pair_grad = jnp.concatenate(pair_grads, axis=0)
    hidden = jnp.concatenate(hiddens, axis=0)

    scales = [
        lax.shift_left(jnp.int32(1), exp_ref[k]).astype(F32) * (1.0 / math.sqrt(128.0))
        for k in range(3)
    ]
    order = [(0, 0), (0, 1), (1, 0), (1, 1), (0, 2), (1, 2)]
    table = had[...]
    for jj in range(blocks // 2):
        at = slice(256 * jj, 256 * jj + 256)
        grads = jnp.concatenate(
            [dot_nn(pair_grad, normed[:, at]), dot_nn(hidden, og_ref[:, at])], axis=0
        )
        bits = pair(sign_ref, first_block + 2 * jj)
        signed = grads * (2 * bits - 1).astype(F32)
        rotated = split_dot(dot_nn, signed, table, True)
        for index, (g, k) in enumerate(order):
            piece = rotated[index * rows_w : (index + 1) * rows_w] * scales[k]
            piece = jnp.clip(piece, -127.0, 127.0).astype(BF16)
            for b in range(2):
                for i in range(groups):
                    unit_at = (2 * jj + b) * per_block + k * groups + i
                    terms[g, unit_at] = piece[16 * i : 16 * i + 16, 128 * b : 128 * b + 128]

    core_copy = remote(terms.at[:, pl.ds(half * (1 - core), half)], core_in, to_core)
    send(core_copy)
    column[1] = to_column(row_total / float(2 * cols))
    core_copy.wait_recv()
    core_sum[...] = (
        terms[:, pl.ds(half * core, half)].astype(F32) + core_in[...].astype(F32)
    ).astype(BF16)
    y_copy = remote(core_sum.at[:, pl.ds(quarter * (1 - y), quarter)], y_in, to_y)
    send(y_copy)

    turned = pair_grad.astype(F32).T.astype(BF16)
    row_mean = column[1]
    row_mean = jnp.concatenate([row_mean, row_mean], axis=1)
    inverse = jnp.concatenate([column[0], column[0]], axis=1)
    for jj in range(blocks // 2):
        at = slice(256 * jj, 256 * jj + 256)
        normed_grad = jnp.zeros((res_ref.shape[0], 256), F32)
        for g in range(2):
            weights = wbuf[g, :2, :, at].reshape(2 * rows_w, 256)
            term = dot_nn(turned[:, 2 * rows_w * g : 2 * rows_w * (g + 1)], weights)
            normed_grad = normed_grad + term.astype(BF16).astype(F32)
        feature_grad = normed_grad * pair(gain_ref, first_block + 2 * jj)
        unit = res_ref[:, at].astype(F32) * inverse
        rg_ref[:, at] = (
            og_ref[:, at].astype(F32) + inverse * (feature_grad - unit * row_mean)
        ).astype(BF16)

    y_copy.wait_recv()
    y_sum[...] = (
        core_sum[:, pl.ds(quarter * y, quarter)].astype(F32) + y_in[...].astype(F32)
    ).astype(BF16)
    z_copies = []
    for o in (1, 2, 3):
        begin = quarter * z_near[o] // 4
        z_copies.append(remote(y_sum.at[:, pl.ds(begin, window)], z_in.at[o - 1], to_z[o]))
        send(z_copies[-1])
    own_begin = quarter * z // 4
    summed = y_sum[:, pl.ds(own_begin, window)].astype(F32)
    for o in (1, 2, 3):
        z_copies[o - 1].wait_recv()
        summed = summed + z_in[o - 1].astype(F32)
    flat = summed.astype(BF16).reshape(2 * window * 16, 128)
    restored = dot_nn(flat, had[:128, :128]).reshape(2, window, 16, 128)
    base = half * core + quarter * y + own_begin
    for i in range(window):
        unit_at = base + i
        bits = sign_ref[first_block + unit_at // per_block]
        exponent = exp_ref[unit_at % per_block // groups]
        factor = lax.shift_left(jnp.int32(1), 30 - exponent).astype(F32) * (
            2.0**-30 / n_dp / math.sqrt(128.0)
        )
        turn = (2 * bits - 1).astype(F32) * factor
        for g in range(2):
            share[g, i] = (restored[g, i] * turn).astype(BF16)

    x_copy = remote(share.at[other], slots.at[me, side], to_x)
    send(x_copy)
    slots[me, side] = share[side]
    x_copy.wait_recv()
    z_copies, y_copies, c_copies = ([], [], [])
    for o in (1, 2, 3):
        z_copies.append(remote(slots.at[me], slots.at[me], to_z[o]))
        send(z_copies[-1])
    for o in range(4):
        slot = z_near[o] * 4 + y * 2 + core
        if o:
            z_copies[o - 1].wait_recv()
        y_copies.append(remote(slots.at[slot], slots.at[slot], to_y))
        send(y_copies[-1])
        c_copies.append(remote(slots.at[slot], slots.at[slot], to_core))
        send(c_copies[-1])
    for o in range(4):
        slot = z_near[o] * 4 + (1 - y) * 2 + core
        y_copies[o].wait_recv()
        c_copies.append(remote(slots.at[slot], slots.at[slot], to_core))
        send(c_copies[-1])
    for copy in c_copies:
        copy.wait_recv()
    for slot in range(n_dp):
        zz, yy, cc = (slot // 4, slot // 2 % 2, slot % 2)
        for i in range(window):
            if zz < 3 and starts[zz] + i >= starts[zz + 1]:
                continue
            unit_at = half * cc + quarter * yy + starts[zz] + i
            block, rest = divmod(unit_at, per_block)
            k, group = divmod(rest, groups)
            for fh in range(2):
                lane = (fh * blocks + block) * 128
                out_ref[k, 16 * group : 16 * group + 16, lane : lane + 128] = slots[slot, fh, i]
    for copy in started:
        copy.wait_send()


COPIES = 30


def fused(n_dp, residual, out_grad, ffn_weights, norm_gain, exponents, sign_bits):
    tokens, cols = residual.shape
    bucket = ffn_weights.shape[1]
    blocks, groups = (cols // 128, bucket // 16)
    units = blocks * 3 * groups
    quarter = units // 4
    starts = [quarter * zz // 4 for zz in range(4)]
    window = -(-quarter // 4)
    vmem = pl.BlockSpec(memory_space=pltpu.VMEM)
    unit = (16, 128)
    scratch = [
        pltpu.VMEM((256, 256), BF16),
        pltpu.VMEM((tokens, cols), BF16),
        pltpu.VMEM((2, tokens, 128), F32),
        pltpu.VMEM((2, 3, bucket, cols), BF16),
        pltpu.VMEM((8, tokens), F32),
        pltpu.VMEM((8, tokens), F32),
        pltpu.VMEM((2, 3 * bucket, tokens), F32),
        pltpu.VMEM((2, 3 * bucket, tokens), BF16),
        pltpu.VMEM((2, 3 * bucket, tokens), BF16),
        pltpu.VMEM((2, units) + unit, BF16),
        pltpu.VMEM((2, units // 2) + unit, BF16),
        pltpu.VMEM((2, units // 2) + unit, BF16),
        pltpu.VMEM((2, quarter) + unit, BF16),
        pltpu.VMEM((2, quarter) + unit, BF16),
        pltpu.VMEM((3, 2, window) + unit, BF16),
        pltpu.VMEM((2, window) + unit, BF16),
        pltpu.VMEM((n_dp, 2, window) + unit, BF16),
        pltpu.SemaphoreType.DMA,
        pltpu.SemaphoreType.DMA((COPIES,)),
        pltpu.SemaphoreType.DMA((COPIES,)),
    ]
    return pl.pallas_call(
        functools.partial(kernel, (n_dp, blocks, groups, window, starts)),
        out_shape=(
            jax.ShapeDtypeStruct((tokens, cols), BF16),
            jax.ShapeDtypeStruct(ffn_weights.shape, BF16),
        ),
        in_specs=[
            vmem,
            vmem,
            pl.BlockSpec(memory_space=pl.ANY),
            vmem,
            pl.BlockSpec(memory_space=pltpu.SMEM),
            vmem,
        ],
        out_specs=(vmem, vmem),
        scratch_shapes=scratch,
        compiler_params=pltpu.CompilerParams(
            collective_id=0, has_side_effects=True, vmem_limit_bytes=48 * 2**20
        ),
    )(
        residual,
        out_grad,
        ffn_weights,
        norm_gain.reshape(-1, 1, 128),
        exponents,
        sign_bits.reshape(-1, 1, 128),
    )


def hadamard():
    indices = jnp.arange(128, dtype=jnp.int32)
    anded = jnp.bitwise_and(indices[:, None], indices[None, :])
    parity = jnp.zeros((128, 128), jnp.int32)
    for offset in range(7):
        parity = parity + jnp.bitwise_and(jnp.right_shift(anded, offset), 1)
    return (1 - 2 * (parity % 2)).astype(jnp.float32) / math.sqrt(128.0)


def gelu_parts(values):
    tanh_input = 0.7978845608 * (values + 0.044715 * values * values * values)
    tanhed = jnp.tanh(tanh_input)
    forward = 0.5 * values * (1.0 + tanhed)
    gelu_slope = 0.5 * (1.0 + tanhed) + 0.5 * values * (1.0 - tanhed * tanhed) * 0.7978845608 * (
        1.0 + 3.0 * 0.044715 * values * values
    )
    return (forward, gelu_slope)


def restore(summed, factors, sign_table, hadamard_table):
    block_count = sign_table.shape[0]
    widened = lax.optimization_barrier(summed).astype(jnp.float32).reshape(3, -1, block_count, 128)
    scaled = widened * factors[:, None, None, None]
    restored = (
        jnp.einsum("kubj,jc->kubc", scaled, hadamard_table, precision=lax.Precision.HIGHEST)
        * sign_table
    )
    return restored.astype(jnp.bfloat16).reshape(3, -1, block_count * 128)


def per_device(residual, out_grad, ffn_weights, norm_gain, exponents, sign_bits):
    full_rows, grads_in = (
        lax.all_gather(residual, "mp", axis=1, tiled=True),
        lax.all_gather(out_grad, "mp", axis=1, tiled=True),
    )
    feature_count = full_rows.shape[1]
    col_count = residual.shape[1]
    col_start = lax.axis_index("mp") * col_count
    bucket_rows = ffn_weights.shape[1]
    rows_wide = full_rows.astype(jnp.float32)
    inverse = lax.rsqrt(jnp.mean(rows_wide * rows_wide, axis=1, keepdims=True) + 1e-06)
    unit_rows = rows_wide * inverse
    normed = (unit_rows * norm_gain).astype(jnp.bfloat16)
    pair_weights = ffn_weights[:2]
    gate_up = jnp.einsum("td,khd->tkh", normed, pair_weights, preferred_element_type=jnp.float32)
    gate_pre = gate_up[:, 0]
    up_proj = gate_up[:, 1]
    activated, gelu_slope = gelu_parts(gate_pre)
    hidden = (activated * up_proj).astype(jnp.bfloat16)
    hidden_grad = lax.dot_general(
        grads_in, ffn_weights[2], (((1,), (1,)), ((), ())), preferred_element_type=jnp.float32
    )
    gate_grad = (hidden_grad * up_proj * gelu_slope).astype(jnp.bfloat16)
    up_grad = (hidden_grad * activated).astype(jnp.bfloat16)
    pair_grad = jnp.stack([gate_grad, up_grad], axis=1)
    partial_value = jnp.einsum(
        "tkh,khd->td", pair_grad, pair_weights, preferred_element_type=jnp.float32
    )
    own_unit = lax.dynamic_slice_in_dim(unit_rows, col_start, col_count, 1)
    normed_grad = lax.psum(partial_value.astype(jnp.bfloat16), "mp").astype(jnp.float32)
    feature_grad = normed_grad * norm_gain
    row_mean = jnp.sum(feature_grad * unit_rows, axis=1, keepdims=True) / feature_count
    own_grad = lax.dynamic_slice_in_dim(feature_grad, col_start, col_count, 1)
    resid_grad = (out_grad.astype(jnp.float32) + inverse * (own_grad - own_unit * row_mean)).astype(
        jnp.bfloat16
    )
    pair_wgrad = jnp.einsum("tkh,td->khd", pair_grad, normed, preferred_element_type=jnp.float32)
    down_wgrad = lax.dot_general(
        hidden, grads_in, (((0,), (0,)), ((), ())), preferred_element_type=jnp.float32
    )
    stacked = jnp.concatenate([pair_wgrad, down_wgrad[None]], axis=0)
    block_count = feature_count // 128
    sign_table = (2 * sign_bits - 1).astype(jnp.float32).reshape(block_count, 128)
    hadamard_table = hadamard()
    shaped = stacked.reshape(3, bucket_rows, block_count, 128) * sign_table
    rotated = jnp.einsum("kubj,jc->kubc", shaped, hadamard_table, precision=lax.Precision.HIGHEST)
    scales = jnp.exp2(exponents.astype(jnp.float32))
    quantized = jnp.clip(rotated * scales[:, None, None, None], -127.0, 127.0).astype(jnp.bfloat16)
    flat_terms = lax.optimization_barrier(quantized).astype(jnp.float32).reshape(-1, 128)
    factors = jnp.exp2(-exponents.astype(jnp.float32)) / float(lax.axis_size("dp"))
    own_share = lax.psum_scatter(flat_terms, "dp", scatter_dimension=0, tiled=True).astype(
        jnp.bfloat16
    )
    gathered = lax.all_gather(own_share, "dp", axis=0, tiled=True)
    weight_grads = restore(gathered, factors, sign_table, hadamard_table)
    return (resid_grad, weight_grads)


def dispatch(n_dp, n_mp, *args):
    cols = args[0].shape[1]
    bucket = args[2].shape[1]
    whole = cols % 256 == 0 and bucket % 32 == 0 and cols // 128 * 3 * (bucket // 16) % 4 == 0
    if n_dp == 16 and n_mp == 2 and whole:
        return fused(n_dp, *args)
    return per_device(*args)


def solution(mesh):
    placed = (P("dp", "mp"), P("dp", "mp"), P(None, "mp", None), P(), P(), P())
    return jax.shard_map(
        functools.partial(dispatch, mesh.shape["dp"], mesh.shape["mp"]),
        mesh=mesh,
        in_specs=placed,
        out_specs=(P("dp", "mp"), P(None, "mp", None)),
        check_vma=False,
    )
```

```python
import functools
import math

import jax
import jax.numpy as jnp
from jax import lax
from jax.experimental import pallas as pl
from jax.experimental.pallas import tpu as pltpu
from jax.sharding import PartitionSpec as P

MESH = pl.DeviceIdType.MESH
F32 = jnp.float32
BF16 = jnp.bfloat16


def dot_nt(left, right):
    return lax.dot_general(left, right, (((1,), (1,)), ((), ())), preferred_element_type=F32)


def dot_nn(left, right):
    return lax.dot_general(left, right, (((1,), (0,)), ((), ())), preferred_element_type=F32)


def split_dot(dot, left, right, split_left):
    wide = left if split_left else right
    high = wide.astype(BF16)
    low = (wide - high.astype(F32)).astype(BF16)
    if split_left:
        return dot(high, right) + dot(low, right)
    return dot(left, high) + dot(left, low)


def signs_256():
    rows = lax.broadcasted_iota(jnp.int32, (256, 256), 0)
    cols = lax.broadcasted_iota(jnp.int32, (256, 256), 1)
    anded = jnp.bitwise_and(jnp.bitwise_and(rows, cols), 127)
    for shift in (4, 2, 1):
        anded = jnp.bitwise_xor(anded, jnp.right_shift(anded, shift))
    value = 1 - 2 * jnp.bitwise_and(anded, 1)
    same = jnp.right_shift(rows, 7) == jnp.right_shift(cols, 7)
    return jnp.where(same, value, 0).astype(F32).astype(BF16)


def to_column(row):
    return jnp.broadcast_to(row[0:1], (128, row.shape[1])).T


def pair(ref, first):
    return jnp.concatenate([ref[pl.ds(first, 1)], ref[pl.ds(first + 1, 1)]], axis=1)


def kernel(
    sizes,
    res_hbm,
    og_hbm,
    w_ref,
    gain_in,
    exp_ref,
    sign_in,
    rg_ref,
    out_ref,
    res_ref,
    og_ref,
    gain_ref,
    sign_ref,
    had,
    normed,
    column,
    wbuf,
    sq_mine,
    sq_peer,
    part,
    part_out,
    part_in,
    *rest,
):
    n_dp, blocks, groups, chunks = sizes
    buffers = rest[:-3]
    local_sem, send_sem, recv_sem = rest[-3:]
    kinds = len(buffers) // len(chunks)
    cols = blocks * 128
    rows_w = 16 * groups
    split = groups // 2
    per_pair = 3 * split
    me = lax.axis_index("dp")
    side = lax.axis_index("mp")
    other = 1 - side
    core = me % 2
    y = (me // 2) % 2
    z = me // 4
    z_near = [z, z + 1 - 2 * (z % 2), (z + 2) % 4, 3 - z]
    first_block = side * blocks
    to_x = (me, other)
    to_core = (me + 1 - 2 * core, side)
    to_y = (me + 2 - 4 * y, side)
    to_z = [None] + [(zz * 4 + y * 2 + core, side) for zz in z_near[1:]]
    started = []

    def send(src, dst, target):
        index = len(started)
        copy = pltpu.make_async_remote_copy(
            src_ref=src,
            dst_ref=dst,
            send_sem=send_sem.at[index],
            recv_sem=recv_sem.at[index],
            device_id=target,
            device_id_type=MESH,
        )
        copy.start()
        started.append(copy)
        return copy

    barrier = pltpu.get_barrier_semaphore()
    partners = [to_x, to_core, to_y] + to_z[1:]
    for target in partners:
        pl.semaphore_signal(barrier, inc=1, device_id=target, device_id_type=MESH)

    own_cols = pl.ds(pl.multiple_of(side * cols, 128), cols)
    peer_cols = pl.ds(pl.multiple_of(other * cols, 128), cols)
    get_res = pltpu.make_async_copy(res_hbm, res_ref, local_sem.at[0])
    get_res.start()
    get_og = pltpu.make_async_copy(og_hbm, og_ref, local_sem.at[1])
    get_og.start()
    get_w = pltpu.make_async_copy(w_ref.at[:, :, own_cols], wbuf.at[side], local_sem.at[2])
    get_w.start()
    had[...] = signs_256()
    gain_ref[...] = gain_in[...]
    sign_ref[...] = (2 * sign_in[...] - 1).astype(F32)
    get_res.wait()
    wide = res_ref[...].astype(F32)
    ones = jnp.ones((8, cols), BF16)
    sq_mine[...] = split_dot(dot_nt, ones, wide * wide, False)
    pl.semaphore_wait(barrier, len(partners))

    sq_copy = send(sq_mine, sq_peer, to_x)
    core_rows = pl.ds(pl.multiple_of(core * (rows_w // 2), 16), rows_w // 2)
    w_copies = {}
    for k in (2, 0, 1):
        w_copies[k] = send(
            w_ref.at[k, core_rows, peer_cols], wbuf.at[side, k, core_rows], to_x
        )

    get_og.wait()
    get_w.wait()
    part[side, 2 * rows_w : 3 * rows_w] = dot_nt(wbuf[side, 2], og_ref[...])
    sq_copy.wait_recv()
    total_sq = sq_mine[...] + sq_peer[...]
    inverse = to_column(lax.rsqrt(total_sq / float(2 * cols) + 1e-06))
    column[0] = inverse
    for j in range(blocks):
        at = slice(128 * j, 128 * j + 128)
        unit = res_ref[:, at].astype(F32) * inverse
        normed[:, at] = (unit * gain_ref[pl.ds(first_block + j, 1)]).astype(BF16)
    part[side, : 2 * rows_w] = dot_nt(
        wbuf[side, :2].reshape(2 * rows_w, cols), normed[...]
    )
    part_out[side] = part[side].astype(BF16)
    own_part = send(part_out.at[side], part_in.at[side], to_x)

    shared = {}
    for k in (2, 0, 1):
        w_copies[k].wait_recv()
        landed = wbuf.at[other, k, core_rows]
        shared[k] = send(landed, landed, to_core)
    shared[2].wait_recv()
    part[other, 2 * rows_w : 3 * rows_w] = dot_nt(wbuf[other, 2], og_ref[...])
    shared[0].wait_recv()
    shared[1].wait_recv()
    part[other, : 2 * rows_w] = dot_nt(
        wbuf[other, :2].reshape(2 * rows_w, cols), normed[...]
    )
    part_out[other] = part[other].astype(BF16)
    peer_part = send(part_out.at[other], part_in.at[other], to_x)
    own_part.wait_recv()
    peer_part.wait_recv()

    pair_grads = []
    hiddens = []
    row_total = jnp.zeros((1, part.shape[2]), F32)
    for g in range(2):
        full = part[g] + part_in[g].astype(F32)
        gate_pre = full[:rows_w]
        up_proj = full[rows_w : 2 * rows_w]
        hidden_grad = full[2 * rows_w :]
        activated, slope = gelu_parts(gate_pre)
        hiddens.append((activated * up_proj).astype(BF16))
        gate_grad = (hidden_grad * up_proj * slope).astype(BF16)
        up_grad = (hidden_grad * activated).astype(BF16)
        pair_grads += [gate_grad, up_grad]
        row_total = row_total + jnp.sum(
            gate_grad.astype(F32) * gate_pre + up_grad.astype(F32) * up_proj,
            axis=0,
            keepdims=True,
        )
    pair_grad = jnp.concatenate(pair_grads, axis=0)
    hidden = jnp.concatenate(hiddens, axis=0)

    scales = [
        lax.shift_left(jnp.int32(1), exp_ref[k]).astype(F32) * (1.0 / math.sqrt(128.0))
        for k in range(3)
    ]
    order = [(0, 0), (0, 1), (1, 0), (1, 1), (0, 2), (1, 2)]

    class Chunk:
        pass

    lanes = []
    for q, (first_pair, pairs, window, starts) in enumerate(chunks):
        chunk = Chunk()
        lanes.append(chunk)
        chunk.first, chunk.pairs, chunk.window, chunk.starts = (
            first_pair,
            pairs,
            window,
            starts,
        )
        chunk.units = pairs * per_pair
        (
            chunk.terms,
            chunk.core_in,
            chunk.core_sum,
            chunk.y_in,
            chunk.y_sum,
            chunk.z_in,
            chunk.share,
            chunk.slots,
        ) = buffers[q * kinds : (q + 1) * kinds]

    def make_terms(chunk):
        table = had[...]
        for jj in range(chunk.first, chunk.first + chunk.pairs):
            at = slice(256 * jj, 256 * jj + 256)
            grads = jnp.concatenate(
                [dot_nn(pair_grad, normed[:, at]), dot_nn(hidden, og_ref[:, at])], axis=0
            )
            signed = grads * pair(sign_ref, first_block + 2 * jj)
            rotated = split_dot(dot_nn, signed, table, True)
            for index, (g, k) in enumerate(order):
                piece = rotated[index * rows_w : (index + 1) * rows_w] * scales[k]
                piece = jnp.clip(piece, -127.0, 127.0).astype(BF16)
                for b in range(2):
                    for i in range(groups):
                        unit_at = (jj - chunk.first) * per_pair + k * split + i % split
                        chunk.terms[i // split, b, g, unit_at] = piece[
                            16 * i : 16 * i + 16, 128 * b : 128 * b + 128
                        ]
        chunk.core_copy = send(chunk.terms.at[1 - core], chunk.core_in, to_core)

    def after_core(chunk):
        chunk.core_copy.wait_recv()
        chunk.core_sum[...] = (
            chunk.terms[core].astype(F32) + chunk.core_in[...].astype(F32)
        ).astype(BF16)
        chunk.y_copy = send(chunk.core_sum.at[1 - y], chunk.y_in, to_y)

    def after_y(chunk):
        chunk.y_copy.wait_recv()
        chunk.y_sum[...] = (
            chunk.core_sum[y].astype(F32) + chunk.y_in[...].astype(F32)
        ).astype(BF16)
        chunk.z_copies = []
        for o in (1, 2, 3):
            begin = chunk.units * z_near[o] // 4
            chunk.z_copies.append(
                send(chunk.y_sum.at[:, pl.ds(begin, chunk.window)], chunk.z_in.at[o - 1], to_z[o])
            )

    def after_z(chunk):
        window = chunk.window
        begin = chunk.units * z // 4
        summed = chunk.y_sum[:, pl.ds(begin, window)].astype(F32)
        for o in (1, 2, 3):
            chunk.z_copies[o - 1].wait_recv()
            summed = summed + chunk.z_in[o - 1].astype(F32)
        flat = summed.astype(BF16).reshape(2 * window * 16, 128)
        restored = dot_nn(flat, had[:128, :128]).reshape(2, window, 16, 128)
        for i in range(window):
            unit_at = begin + i
            block = 2 * (chunk.first + unit_at // per_pair) + y
            exponent = exp_ref[unit_at % per_pair // split]
            factor = lax.shift_left(jnp.int32(1), 30 - exponent).astype(F32) * (
                2.0**-30 / n_dp / math.sqrt(128.0)
            )
            turn = sign_ref[pl.ds(first_block + block, 1)] * factor
            for g in range(2):
                chunk.share[g, i] = (restored[g, i] * turn).astype(BF16)
        chunk.x_copy = send(chunk.share.at[other], chunk.slots.at[me, side], to_x)
        chunk.slots[me, side] = chunk.share[side]

    def forward(chunk, slot, targets):
        block = chunk.slots.at[slot]
        return [send(block, block, target) for target in targets]

    def after_x(chunk):
        chunk.x_copy.wait_recv()
        chunk.z_copies = forward(chunk, me, to_z[1:])
        to_both = forward(chunk, me, [to_y, to_core])
        chunk.y_copies = to_both[:1]
        chunk.c_copies = to_both[1:]

    def gather_z(chunk):
        for o in (1, 2, 3):
            chunk.z_copies[o - 1].wait_recv()
            to_both = forward(chunk, z_near[o] * 4 + y * 2 + core, [to_y, to_core])
            chunk.y_copies.append(to_both[0])
            chunk.c_copies.append(to_both[1])

    def gather_y(chunk):
        for o in range(4):
            chunk.y_copies[o].wait_recv()
            chunk.c_copies += forward(
                chunk, z_near[o] * 4 + (1 - y) * 2 + core, [to_core]
            )

    def assemble(chunk):
        for copy in chunk.c_copies:
            copy.wait_recv()
        for slot in range(n_dp):
            zz, yy, cc = (slot // 4, slot // 2 % 2, slot % 2)
            for i in range(chunk.window):
                unit_at = chunk.starts[zz] + i
                if zz < 3 and unit_at >= chunk.starts[zz + 1]:
                    continue
                pair_at, rest_at = divmod(unit_at, per_pair)
                block = 2 * (chunk.first + pair_at) + yy
                k = rest_at // split
                top = 16 * (cc * split + rest_at % split)
                for fh in range(2):
                    lane = (fh * blocks + block) * 128
                    out_ref[k, top : top + 16, lane : lane + 128] = chunk.slots[slot, fh, i]

    def make_resid(first_pair, last_pair):
        row_mean = jnp.concatenate([column[1], column[1]], axis=1)
        inverse = jnp.concatenate([column[0], column[0]], axis=1)
        for jj in range(first_pair, last_pair):
            at = slice(256 * jj, 256 * jj + 256)
            normed_grad = jnp.zeros((res_ref.shape[0], 256), F32)
            for g in range(2):
                weights = wbuf[g, :2, :, at].reshape(2 * rows_w, 256)
                term = dot_nn(turned[:, 2 * rows_w * g : 2 * rows_w * (g + 1)], weights)
                normed_grad = normed_grad + term.astype(BF16).astype(F32)
            feature_grad = normed_grad * pair(gain_ref, first_block + 2 * jj)
            unit = res_ref[:, at].astype(F32) * inverse
            rg_ref[:, at] = (
                og_ref[:, at].astype(F32) + inverse * (feature_grad - unit * row_mean)
            ).astype(BF16)

    one, two = lanes
    all_pairs = blocks // 2
    make_terms(one)
    make_terms(two)
    after_core(one)
    column[1] = to_column(row_total / float(2 * cols))
    turned = pair_grad.astype(F32).T.astype(BF16)
    after_core(two)
    make_resid(0, all_pairs // 3)
    after_y(one)
    make_resid(all_pairs // 3, 2 * all_pairs // 3)
    after_y(two)
    after_z(one)
    make_resid(2 * all_pairs // 3, all_pairs)
    after_x(one)
    after_z(two)
    gather_z(one)
    after_x(two)
    gather_y(one)
    gather_z(two)
    gather_y(two)
    assemble(one)
    assemble(two)
    for copy in started:
        copy.wait_send()


COPIES = 9 + 2 * 21


def fused(n_dp, residual, out_grad, ffn_weights, norm_gain, exponents, sign_bits):
    tokens, cols = residual.shape
    bucket = ffn_weights.shape[1]
    blocks, groups = (cols // 128, bucket // 16)
    all_pairs = blocks // 2
    per_pair = 3 * groups // 2
    cut = all_pairs // 2
    vmem = pl.BlockSpec(memory_space=pltpu.VMEM)
    hbm = pl.BlockSpec(memory_space=pltpu.HBM)
    scratch = [
        pltpu.VMEM((tokens, cols), BF16),
        pltpu.VMEM((tokens, cols), BF16),
        pltpu.VMEM((2 * blocks, 128), F32),
        pltpu.VMEM((2 * blocks, 128), F32),
        pltpu.VMEM((256, 256), BF16),
        pltpu.VMEM((tokens, cols), BF16),
        pltpu.VMEM((2, tokens, 128), F32),
        pltpu.VMEM((2, 3, bucket, cols), BF16),
        pltpu.VMEM((8, tokens), F32),
        pltpu.VMEM((8, tokens), F32),
        pltpu.VMEM((2, 3 * bucket, tokens), F32),
        pltpu.VMEM((2, 3 * bucket, tokens), BF16),
        pltpu.VMEM((2, 3 * bucket, tokens), BF16),
    ]
    chunks = []
    for first, pairs in ((0, cut), (cut, all_pairs - cut)):
        units = pairs * per_pair
        window = -(-units // 4)
        chunks.append((first, pairs, window, [units * zz // 4 for zz in range(4)]))
        for lead in (
            (2, 2, 2, units),
            (2, 2, units),
            (2, 2, units),
            (2, units),
            (2, units),
            (3, 2, window),
            (2, window),
            (n_dp, 2, window),
        ):
            scratch.append(pltpu.VMEM(lead + (16, 128), BF16))
    scratch += [
        pltpu.SemaphoreType.DMA((3,)),
        pltpu.SemaphoreType.DMA((COPIES,)),
        pltpu.SemaphoreType.DMA((COPIES,)),
    ]
    return pl.pallas_call(
        functools.partial(kernel, (n_dp, blocks, groups, chunks)),
        out_shape=(
            pltpu.VMEM((tokens, cols), BF16),
            pltpu.VMEM(ffn_weights.shape, BF16),
        ),
        in_specs=[
            hbm,
            hbm,
            hbm,
            vmem,
            pl.BlockSpec(memory_space=pltpu.SMEM),
            vmem,
        ],
        out_specs=(vmem, vmem),
        scratch_shapes=scratch,
        compiler_params=pltpu.CompilerParams(
            collective_id=0, has_side_effects=True, vmem_limit_bytes=58 * 2**20
        ),
    )(
        residual,
        out_grad,
        ffn_weights,
        norm_gain.reshape(-1, 128),
        exponents,
        sign_bits.reshape(-1, 128),
    )


def hadamard():
    indices = jnp.arange(128, dtype=jnp.int32)
    anded = jnp.bitwise_and(indices[:, None], indices[None, :])
    parity = jnp.zeros((128, 128), jnp.int32)
    for offset in range(7):
        parity = parity + jnp.bitwise_and(jnp.right_shift(anded, offset), 1)
    return (1 - 2 * (parity % 2)).astype(jnp.float32) / math.sqrt(128.0)


def gelu_parts(values):
    tanh_input = 0.7978845608 * (values + 0.044715 * values * values * values)
    tanhed = jnp.tanh(tanh_input)
    forward = 0.5 * values * (1.0 + tanhed)
    gelu_slope = 0.5 * (1.0 + tanhed) + 0.5 * values * (1.0 - tanhed * tanhed) * 0.7978845608 * (
        1.0 + 3.0 * 0.044715 * values * values
    )
    return (forward, gelu_slope)


def restore(summed, factors, sign_table, hadamard_table):
    block_count = sign_table.shape[0]
    widened = lax.optimization_barrier(summed).astype(jnp.float32).reshape(3, -1, block_count, 128)
    scaled = widened * factors[:, None, None, None]
    restored = (
        jnp.einsum("kubj,jc->kubc", scaled, hadamard_table, precision=lax.Precision.HIGHEST)
        * sign_table
    )
    return restored.astype(jnp.bfloat16).reshape(3, -1, block_count * 128)


def per_device(residual, out_grad, ffn_weights, norm_gain, exponents, sign_bits):
    full_rows, grads_in = (
        lax.all_gather(residual, "mp", axis=1, tiled=True),
        lax.all_gather(out_grad, "mp", axis=1, tiled=True),
    )
    feature_count = full_rows.shape[1]
    col_count = residual.shape[1]
    col_start = lax.axis_index("mp") * col_count
    bucket_rows = ffn_weights.shape[1]
    rows_wide = full_rows.astype(jnp.float32)
    inverse = lax.rsqrt(jnp.mean(rows_wide * rows_wide, axis=1, keepdims=True) + 1e-06)
    unit_rows = rows_wide * inverse
    normed = (unit_rows * norm_gain).astype(jnp.bfloat16)
    pair_weights = ffn_weights[:2]
    gate_up = jnp.einsum("td,khd->tkh", normed, pair_weights, preferred_element_type=jnp.float32)
    gate_pre = gate_up[:, 0]
    up_proj = gate_up[:, 1]
    activated, gelu_slope = gelu_parts(gate_pre)
    hidden = (activated * up_proj).astype(jnp.bfloat16)
    hidden_grad = lax.dot_general(
        grads_in, ffn_weights[2], (((1,), (1,)), ((), ())), preferred_element_type=jnp.float32
    )
    gate_grad = (hidden_grad * up_proj * gelu_slope).astype(jnp.bfloat16)
    up_grad = (hidden_grad * activated).astype(jnp.bfloat16)
    pair_grad = jnp.stack([gate_grad, up_grad], axis=1)
    partial_value = jnp.einsum(
        "tkh,khd->td", pair_grad, pair_weights, preferred_element_type=jnp.float32
    )
    own_unit = lax.dynamic_slice_in_dim(unit_rows, col_start, col_count, 1)
    normed_grad = lax.psum(partial_value.astype(jnp.bfloat16), "mp").astype(jnp.float32)
    feature_grad = normed_grad * norm_gain
    row_mean = jnp.sum(feature_grad * unit_rows, axis=1, keepdims=True) / feature_count
    own_grad = lax.dynamic_slice_in_dim(feature_grad, col_start, col_count, 1)
    resid_grad = (out_grad.astype(jnp.float32) + inverse * (own_grad - own_unit * row_mean)).astype(
        jnp.bfloat16
    )
    pair_wgrad = jnp.einsum("tkh,td->khd", pair_grad, normed, preferred_element_type=jnp.float32)
    down_wgrad = lax.dot_general(
        hidden, grads_in, (((0,), (0,)), ((), ())), preferred_element_type=jnp.float32
    )
    stacked = jnp.concatenate([pair_wgrad, down_wgrad[None]], axis=0)
    block_count = feature_count // 128
    sign_table = (2 * sign_bits - 1).astype(jnp.float32).reshape(block_count, 128)
    hadamard_table = hadamard()
    shaped = stacked.reshape(3, bucket_rows, block_count, 128) * sign_table
    rotated = jnp.einsum("kubj,jc->kubc", shaped, hadamard_table, precision=lax.Precision.HIGHEST)
    scales = jnp.exp2(exponents.astype(jnp.float32))
    quantized = jnp.clip(rotated * scales[:, None, None, None], -127.0, 127.0).astype(jnp.bfloat16)
    flat_terms = lax.optimization_barrier(quantized).astype(jnp.float32).reshape(-1, 128)
    factors = jnp.exp2(-exponents.astype(jnp.float32)) / float(lax.axis_size("dp"))
    own_share = lax.psum_scatter(flat_terms, "dp", scatter_dimension=0, tiled=True).astype(
        jnp.bfloat16
    )
    gathered = lax.all_gather(own_share, "dp", axis=0, tiled=True)
    weight_grads = restore(gathered, factors, sign_table, hadamard_table)
    return (resid_grad, weight_grads)


def dispatch(n_dp, n_mp, *args):
    cols = args[0].shape[1]
    bucket = args[2].shape[1]
    whole = cols % 256 == 0 and bucket % 32 == 0 and cols >= 512
    if n_dp == 16 and n_mp == 2 and whole:
        return fused(n_dp, *args)
    return per_device(*args)


def solution(mesh):
    placed = (P("dp", "mp"), P("dp", "mp"), P(None, "mp", None), P(), P(), P())
    return jax.shard_map(
        functools.partial(dispatch, mesh.shape["dp"], mesh.shape["mp"]),
        mesh=mesh,
        in_specs=placed,
        out_specs=(P("dp", "mp"), P(None, "mp", None)),
        check_vma=False,
    )
```

```python
import functools
import math

import jax
import jax.numpy as jnp
from jax import lax
from jax.experimental import pallas as pl
from jax.experimental.pallas import tpu as pltpu
from jax.sharding import PartitionSpec as P

MESH = pl.DeviceIdType.MESH
F32 = jnp.float32
BF16 = jnp.bfloat16


def dot_nn(left, right):
    return lax.dot_general(left, right, (((1,), (0,)), ((), ())), preferred_element_type=F32)


def split_dot(left, right):
    high = left.astype(BF16)
    low = (left - high.astype(F32)).astype(BF16)
    return dot_nn(high, right) + dot_nn(low, right)


def signs_256():
    rows = lax.broadcasted_iota(jnp.int32, (256, 256), 0)
    cols = lax.broadcasted_iota(jnp.int32, (256, 256), 1)
    anded = jnp.bitwise_and(jnp.bitwise_and(rows, cols), 127)
    for shift in (4, 2, 1):
        anded = jnp.bitwise_xor(anded, jnp.right_shift(anded, shift))
    value = 1 - 2 * jnp.bitwise_and(anded, 1)
    same = jnp.right_shift(rows, 7) == jnp.right_shift(cols, 7)
    return jnp.where(same, value, 0).astype(F32).astype(BF16)


def to_column(row):
    return jnp.broadcast_to(row[0:1], (128, row.shape[1])).T


def pair(ref, first):
    return jnp.concatenate([ref[pl.ds(first, 1)], ref[pl.ds(first + 1, 1)]], axis=1)


def kernel(
    sizes,
    res_hbm,
    og_hbm,
    w_ref,
    gain_in,
    exp_ref,
    sign_in,
    rg_ref,
    out_ref,
    res_ref,
    og_ref,
    gain_ref,
    sign_ref,
    had,
    normed,
    column,
    wbuf,
    og_turned,
    normed_turned,
    sq_mine,
    sq_peer,
    part,
    part_out,
    part_in,
    *rest,
):
    n_dp, blocks, groups, chunks = sizes
    buffers = rest[:-3]
    local_sem, send_sem, recv_sem = rest[-3:]
    kinds = len(buffers) // len(chunks)
    cols = blocks * 128
    rows_w = 16 * groups
    split = groups // 2
    per_pair = 3 * split
    me = lax.axis_index("dp")
    side = lax.axis_index("mp")
    other = 1 - side
    core = me % 2
    y = (me // 2) % 2
    z = me // 4
    z_near = [z, z + 1 - 2 * (z % 2), (z + 2) % 4, 3 - z]
    first_block = side * blocks
    to_x = (me, other)
    to_core = (me + 1 - 2 * core, side)
    to_y = (me + 2 - 4 * y, side)
    to_z = [None] + [(zz * 4 + y * 2 + core, side) for zz in z_near[1:]]
    started = []

    def send(src, dst, target):
        index = len(started)
        copy = pltpu.make_async_remote_copy(
            src_ref=src,
            dst_ref=dst,
            send_sem=send_sem.at[index],
            recv_sem=recv_sem.at[index],
            device_id=target,
            device_id_type=MESH,
        )
        copy.start()
        started.append(copy)
        return copy

    barrier = pltpu.get_barrier_semaphore()
    partners = [to_x, to_core, to_y] + to_z[1:]
    for target in partners:
        pl.semaphore_signal(barrier, inc=1, device_id=target, device_id_type=MESH)

    own_cols = pl.ds(pl.multiple_of(side * cols, 128), cols)
    get_res = pltpu.make_async_copy(res_hbm, res_ref, local_sem.at[0])
    get_res.start()
    get_og = pltpu.make_async_copy(og_hbm, og_ref, local_sem.at[1])
    get_og.start()
    get_w = pltpu.make_async_copy(w_ref.at[:, :, own_cols], wbuf.at[side], local_sem.at[2])
    get_w.start()
    had[...] = signs_256()
    gain_ref[...] = gain_in[...]
    sign_ref[...] = (2 * sign_in[...] - 1).astype(F32)
    core_rows = pl.ds(pl.multiple_of(core * (rows_w // 2), 16), rows_w // 2)
    pieces = 3
    cuts = [256 * (blocks // 2 * p // pieces) for p in range(pieces + 1)]

    def send_w(p):
        width = cuts[p + 1] - cuts[p]
        from_cols = pl.ds(pl.multiple_of(other * cols + cuts[p], 128), width)
        return send(
            w_ref.at[:, core_rows, from_cols],
            wbuf.at[side, :, core_rows, pl.ds(cuts[p], width)],
            to_x,
        )

    pl.semaphore_wait(barrier, len(partners))
    w_copies = [send_w(0), send_w(1)]
    get_res.wait()
    squares = jnp.zeros(column.shape[1:], F32)
    for j in range(blocks):
        wide = res_ref[:, 128 * j : 128 * j + 128].astype(F32)
        squares = squares + wide * wide
    sums = jnp.sum(squares.T, axis=0, keepdims=True)
    sq_mine[...] = jnp.broadcast_to(sums, sq_mine.shape)
    sq_copy = send(sq_mine, sq_peer, to_x)
    w_copies.append(send_w(2))

    get_og.wait()
    for j in range(blocks):
        at = slice(128 * j, 128 * j + 128)
        og_turned[at] = og_ref[:, at].T
    get_w.wait()
    part[side, 2 * rows_w : 3 * rows_w] = dot_nn(wbuf[side, 2], og_turned[...])
    sq_copy.wait_recv()
    total_sq = sq_mine[...] + sq_peer[...]
    inverse = to_column(lax.rsqrt(total_sq / float(2 * cols) + 1e-06))
    column[0] = inverse
    for j in range(blocks):
        at = slice(128 * j, 128 * j + 128)
        unit = res_ref[:, at].astype(F32) * inverse
        scaled = (unit * gain_ref[pl.ds(first_block + j, 1)]).astype(BF16)
        normed[:, at] = scaled
        normed_turned[at] = scaled.T
    part[side, : 2 * rows_w] = dot_nn(
        wbuf[side, :2].reshape(2 * rows_w, cols), normed_turned[...]
    )
    part_out[side] = part[side].astype(BF16)
    own_part = send(part_out.at[side], part_in.at[side], to_x)

    shared = []
    pair_part = jnp.zeros((2 * rows_w, part.shape[2]), F32)
    down_part = jnp.zeros((rows_w, part.shape[2]), F32)
    for p in range(pieces + 1):
        if p < pieces:
            w_copies[p].wait_recv()
            landed = wbuf.at[other, :, core_rows, pl.ds(cuts[p], cuts[p + 1] - cuts[p])]
            shared.append(send(landed, landed, to_core))
        if p > 0:
            shared[p - 1].wait_recv()
            width = cuts[p] - cuts[p - 1]
            at = slice(cuts[p - 1], cuts[p])
            weights = wbuf[other, :2, :, at].reshape(2 * rows_w, width)
            pair_part = pair_part + dot_nn(weights, normed_turned[at])
            down_part = down_part + dot_nn(wbuf[other, 2, :, at], og_turned[at])
    part[other, : 2 * rows_w] = pair_part
    part[other, 2 * rows_w : 3 * rows_w] = down_part
    part_out[other] = part[other].astype(BF16)
    peer_part = send(part_out.at[other], part_in.at[other], to_x)
    own_part.wait_recv()
    peer_part.wait_recv()

    pair_grads = []
    hiddens = []
    row_total = jnp.zeros((1, part.shape[2]), F32)
    for g in range(2):
        full = part[g] + part_in[g].astype(F32)
        gate_pre = full[:rows_w]
        up_proj = full[rows_w : 2 * rows_w]
        hidden_grad = full[2 * rows_w :]
        activated, slope = gelu_parts(gate_pre)
        hiddens.append((activated * up_proj).astype(BF16))
        gate_grad = (hidden_grad * up_proj * slope).astype(BF16)
        up_grad = (hidden_grad * activated).astype(BF16)
        pair_grads += [gate_grad, up_grad]
        row_total = row_total + jnp.sum(
            gate_grad.astype(F32) * gate_pre + up_grad.astype(F32) * up_proj,
            axis=0,
            keepdims=True,
        )
    pair_grad = jnp.concatenate(pair_grads, axis=0)
    hidden = jnp.concatenate(hiddens, axis=0)

    scales = [
        lax.shift_left(jnp.int32(1), exp_ref[k]).astype(F32) * (1.0 / math.sqrt(128.0))
        for k in range(3)
    ]
    order = [(0, 0), (0, 1), (1, 0), (1, 1), (0, 2), (1, 2)]

    class Chunk:
        pass

    lanes = []
    for q, (first_pair, pairs, window, starts) in enumerate(chunks):
        chunk = Chunk()
        lanes.append(chunk)
        chunk.first, chunk.pairs, chunk.window, chunk.starts = (
            first_pair,
            pairs,
            window,
            starts,
        )
        chunk.units = pairs * per_pair
        (
            chunk.terms,
            chunk.core_in,
            chunk.core_sum,
            chunk.y_in,
            chunk.y_sum,
            chunk.z_in,
            chunk.share,
            chunk.slots,
        ) = buffers[q * kinds : (q + 1) * kinds]

    def make_terms(chunk):
        table = had[...]
        for jj in range(chunk.first, chunk.first + chunk.pairs):
            at = slice(256 * jj, 256 * jj + 256)
            grads = jnp.concatenate(
                [dot_nn(pair_grad, normed[:, at]), dot_nn(hidden, og_ref[:, at])], axis=0
            )
            signed = grads * pair(sign_ref, first_block + 2 * jj)
            rotated = split_dot(signed, table)
            for index, (g, k) in enumerate(order):
                piece = rotated[index * rows_w : (index + 1) * rows_w] * scales[k]
                piece = jnp.clip(piece, -127.0, 127.0).astype(BF16)
                for b in range(2):
                    for i in range(groups):
                        unit_at = (jj - chunk.first) * per_pair + k * split + i % split
                        chunk.terms[i // split, b, g, unit_at] = piece[
                            16 * i : 16 * i + 16, 128 * b : 128 * b + 128
                        ]
        chunk.core_copy = send(chunk.terms.at[1 - core], chunk.core_in, to_core)

    def after_core(chunk):
        chunk.core_copy.wait_recv()
        chunk.core_sum[...] = (
            chunk.terms[core].astype(F32) + chunk.core_in[...].astype(F32)
        ).astype(BF16)
        chunk.y_copy = send(chunk.core_sum.at[1 - y], chunk.y_in, to_y)

    def after_y(chunk):
        chunk.y_copy.wait_recv()
        chunk.y_sum[...] = (
            chunk.core_sum[y].astype(F32) + chunk.y_in[...].astype(F32)
        ).astype(BF16)
        chunk.z_copies = []
        for o in (1, 2, 3):
            begin = chunk.units * z_near[o] // 4
            chunk.z_copies.append(
                send(chunk.y_sum.at[:, pl.ds(begin, chunk.window)], chunk.z_in.at[o - 1], to_z[o])
            )

    def after_z(chunk):
        window = chunk.window
        begin = chunk.units * z // 4
        summed = chunk.y_sum[:, pl.ds(begin, window)].astype(F32)
        for o in (1, 2, 3):
            chunk.z_copies[o - 1].wait_recv()
            summed = summed + chunk.z_in[o - 1].astype(F32)
        flat = summed.astype(BF16).reshape(2 * window * 16, 128)
        restored = dot_nn(flat, had[:128, :128]).reshape(2, window, 16, 128)
        for i in range(window):
            unit_at = begin + i
            block = 2 * (chunk.first + unit_at // per_pair) + y
            exponent = exp_ref[unit_at % per_pair // split]
            factor = lax.shift_left(jnp.int32(1), 30 - exponent).astype(F32) * (
                2.0**-30 / n_dp / math.sqrt(128.0)
            )
            turn = sign_ref[pl.ds(first_block + block, 1)] * factor
            for g in range(2):
                chunk.share[g, i] = (restored[g, i] * turn).astype(BF16)
        chunk.x_copy = send(chunk.share.at[other], chunk.slots.at[me, side], to_x)
        chunk.slots[me, side] = chunk.share[side]

    def forward(chunk, slot, targets):
        block = chunk.slots.at[slot]
        return [send(block, block, target) for target in targets]

    def after_x(chunk):
        chunk.x_copy.wait_recv()
        chunk.z_copies = forward(chunk, me, to_z[1:])
        to_both = forward(chunk, me, [to_y, to_core])
        chunk.y_copies = to_both[:1]
        chunk.c_copies = to_both[1:]

    def gather_z(chunk):
        for o in (1, 2, 3):
            chunk.z_copies[o - 1].wait_recv()
            to_both = forward(chunk, z_near[o] * 4 + y * 2 + core, [to_y, to_core])
            chunk.y_copies.append(to_both[0])
            chunk.c_copies.append(to_both[1])

    def gather_y(chunk):
        for o in range(4):
            chunk.y_copies[o].wait_recv()
            chunk.c_copies += forward(
                chunk, z_near[o] * 4 + (1 - y) * 2 + core, [to_core]
            )

    def assemble(chunk):
        for copy in chunk.c_copies:
            copy.wait_recv()
        for slot in range(n_dp):
            zz, yy, cc = (slot // 4, slot // 2 % 2, slot % 2)
            for i in range(chunk.window):
                unit_at = chunk.starts[zz] + i
                if zz < 3 and unit_at >= chunk.starts[zz + 1]:
                    continue
                pair_at, rest_at = divmod(unit_at, per_pair)
                block = 2 * (chunk.first + pair_at) + yy
                k = rest_at // split
                top = 16 * (cc * split + rest_at % split)
                for fh in range(2):
                    lane = (fh * blocks + block) * 128
                    out_ref[k, top : top + 16, lane : lane + 128] = chunk.slots[slot, fh, i]

    def make_resid(first_pair, last_pair):
        row_mean = jnp.concatenate([column[1], column[1]], axis=1)
        inverse = jnp.concatenate([column[0], column[0]], axis=1)
        for jj in range(first_pair, last_pair):
            at = slice(256 * jj, 256 * jj + 256)
            normed_grad = jnp.zeros((res_ref.shape[0], 256), F32)
            for g in range(2):
                weights = wbuf[g, :2, :, at].reshape(2 * rows_w, 256)
                term = dot_nn(turned[:, 2 * rows_w * g : 2 * rows_w * (g + 1)], weights)
                normed_grad = normed_grad + term.astype(BF16).astype(F32)
            feature_grad = normed_grad * pair(gain_ref, first_block + 2 * jj)
            unit = res_ref[:, at].astype(F32) * inverse
            rg_ref[:, at] = (
                og_ref[:, at].astype(F32) + inverse * (feature_grad - unit * row_mean)
            ).astype(BF16)

    one, two = lanes
    all_pairs = blocks // 2
    make_terms(one)
    make_terms(two)
    after_core(one)
    column[1] = to_column(row_total / float(2 * cols))
    turned = pair_grad.astype(F32).T.astype(BF16)
    after_core(two)
    make_resid(0, all_pairs // 3)
    after_y(one)
    make_resid(all_pairs // 3, 2 * all_pairs // 3)
    after_y(two)
    after_z(one)
    make_resid(2 * all_pairs // 3, all_pairs)
    after_x(one)
    after_z(two)
    gather_z(one)
    after_x(two)
    gather_y(one)
    gather_z(two)
    gather_y(two)
    assemble(one)
    assemble(two)
    for copy in started:
        copy.wait_send()


def write_out(rg_ref, wg_ref, rg_out, wg_out, sems):
    copies = [
        pltpu.make_async_copy(rg_ref, rg_out, sems.at[0]),
        pltpu.make_async_copy(wg_ref, wg_out, sems.at[1]),
    ]
    for copy in copies:
        copy.start()
    for copy in copies:
        copy.wait()


COPIES = 9 + 2 * 21


def fused(n_dp, residual, out_grad, ffn_weights, norm_gain, exponents, sign_bits):
    tokens, cols = residual.shape
    bucket = ffn_weights.shape[1]
    blocks, groups = (cols // 128, bucket // 16)
    all_pairs = blocks // 2
    per_pair = 3 * groups // 2
    cut = all_pairs // 2
    vmem = pl.BlockSpec(memory_space=pltpu.VMEM)
    hbm = pl.BlockSpec(memory_space=pltpu.HBM)
    scratch = [
        pltpu.VMEM((tokens, cols), BF16),
        pltpu.VMEM((tokens, cols), BF16),
        pltpu.VMEM((2 * blocks, 128), F32),
        pltpu.VMEM((2 * blocks, 128), F32),
        pltpu.VMEM((256, 256), BF16),
        pltpu.VMEM((tokens, cols), BF16),
        pltpu.VMEM((2, tokens, 128), F32),
        pltpu.VMEM((2, 3, bucket, cols), BF16),
        pltpu.VMEM((cols, tokens), BF16),
        pltpu.VMEM((cols, tokens), BF16),
        pltpu.VMEM((8, tokens), F32),
        pltpu.VMEM((8, tokens), F32),
        pltpu.VMEM((2, 3 * bucket, tokens), F32),
        pltpu.VMEM((2, 3 * bucket, tokens), BF16),
        pltpu.VMEM((2, 3 * bucket, tokens), BF16),
    ]
    chunks = []
    for first, pairs in ((0, cut), (cut, all_pairs - cut)):
        units = pairs * per_pair
        window = -(-units // 4)
        chunks.append((first, pairs, window, [units * zz // 4 for zz in range(4)]))
        for lead in (
            (2, 2, 2, units),
            (2, 2, units),
            (2, 2, units),
            (2, units),
            (2, units),
            (3, 2, window),
            (2, window),
            (n_dp, 2, window),
        ):
            scratch.append(pltpu.VMEM(lead + (16, 128), BF16))
    scratch += [
        pltpu.SemaphoreType.DMA((3,)),
        pltpu.SemaphoreType.DMA((COPIES,)),
        pltpu.SemaphoreType.DMA((COPIES,)),
    ]
    results = pl.pallas_call(
        functools.partial(kernel, (n_dp, blocks, groups, chunks)),
        out_shape=(
            pltpu.VMEM((tokens, cols), BF16),
            pltpu.VMEM(ffn_weights.shape, BF16),
        ),
        in_specs=[
            hbm,
            hbm,
            hbm,
            vmem,
            pl.BlockSpec(memory_space=pltpu.SMEM),
            vmem,
        ],
        out_specs=(vmem, vmem),
        scratch_shapes=scratch,
        compiler_params=pltpu.CompilerParams(
            collective_id=0, has_side_effects=True, vmem_limit_bytes=58 * 2**20
        ),
    )(
        residual,
        out_grad,
        ffn_weights,
        norm_gain.reshape(-1, 128),
        exponents,
        sign_bits.reshape(-1, 128),
    )
    return pl.pallas_call(
        write_out,
        out_shape=[jax.ShapeDtypeStruct(result.shape, BF16) for result in results],
        in_specs=[vmem, vmem],
        out_specs=[hbm, hbm],
        scratch_shapes=[pltpu.SemaphoreType.DMA((2,))],
    )(*results)


def hadamard():
    indices = jnp.arange(128, dtype=jnp.int32)
    anded = jnp.bitwise_and(indices[:, None], indices[None, :])
    parity = jnp.zeros((128, 128), jnp.int32)
    for offset in range(7):
        parity = parity + jnp.bitwise_and(jnp.right_shift(anded, offset), 1)
    return (1 - 2 * (parity % 2)).astype(jnp.float32) / math.sqrt(128.0)


def gelu_parts(values):
    tanh_input = 0.7978845608 * (values + 0.044715 * values * values * values)
    tanhed = jnp.tanh(tanh_input)
    forward = 0.5 * values * (1.0 + tanhed)
    gelu_slope = 0.5 * (1.0 + tanhed) + 0.5 * values * (1.0 - tanhed * tanhed) * 0.7978845608 * (
        1.0 + 3.0 * 0.044715 * values * values
    )
    return (forward, gelu_slope)


def restore(summed, factors, sign_table, hadamard_table):
    block_count = sign_table.shape[0]
    widened = lax.optimization_barrier(summed).astype(jnp.float32).reshape(3, -1, block_count, 128)
    scaled = widened * factors[:, None, None, None]
    restored = (
        jnp.einsum("kubj,jc->kubc", scaled, hadamard_table, precision=lax.Precision.HIGHEST)
        * sign_table
    )
    return restored.astype(jnp.bfloat16).reshape(3, -1, block_count * 128)


def per_device(residual, out_grad, ffn_weights, norm_gain, exponents, sign_bits):
    full_rows, grads_in = (
        lax.all_gather(residual, "mp", axis=1, tiled=True),
        lax.all_gather(out_grad, "mp", axis=1, tiled=True),
    )
    feature_count = full_rows.shape[1]
    col_count = residual.shape[1]
    col_start = lax.axis_index("mp") * col_count
    bucket_rows = ffn_weights.shape[1]
    rows_wide = full_rows.astype(jnp.float32)
    inverse = lax.rsqrt(jnp.mean(rows_wide * rows_wide, axis=1, keepdims=True) + 1e-06)
    unit_rows = rows_wide * inverse
    normed = (unit_rows * norm_gain).astype(jnp.bfloat16)
    pair_weights = ffn_weights[:2]
    gate_up = jnp.einsum("td,khd->tkh", normed, pair_weights, preferred_element_type=jnp.float32)
    gate_pre = gate_up[:, 0]
    up_proj = gate_up[:, 1]
    activated, gelu_slope = gelu_parts(gate_pre)
    hidden = (activated * up_proj).astype(jnp.bfloat16)
    hidden_grad = lax.dot_general(
        grads_in, ffn_weights[2], (((1,), (1,)), ((), ())), preferred_element_type=jnp.float32
    )
    gate_grad = (hidden_grad * up_proj * gelu_slope).astype(jnp.bfloat16)
    up_grad = (hidden_grad * activated).astype(jnp.bfloat16)
    pair_grad = jnp.stack([gate_grad, up_grad], axis=1)
    partial_value = jnp.einsum(
        "tkh,khd->td", pair_grad, pair_weights, preferred_element_type=jnp.float32
    )
    own_unit = lax.dynamic_slice_in_dim(unit_rows, col_start, col_count, 1)
    normed_grad = lax.psum(partial_value.astype(jnp.bfloat16), "mp").astype(jnp.float32)
    feature_grad = normed_grad * norm_gain
    row_mean = jnp.sum(feature_grad * unit_rows, axis=1, keepdims=True) / feature_count
    own_grad = lax.dynamic_slice_in_dim(feature_grad, col_start, col_count, 1)
    resid_grad = (out_grad.astype(jnp.float32) + inverse * (own_grad - own_unit * row_mean)).astype(
        jnp.bfloat16
    )
    pair_wgrad = jnp.einsum("tkh,td->khd", pair_grad, normed, preferred_element_type=jnp.float32)
    down_wgrad = lax.dot_general(
        hidden, grads_in, (((0,), (0,)), ((), ())), preferred_element_type=jnp.float32
    )
    stacked = jnp.concatenate([pair_wgrad, down_wgrad[None]], axis=0)
    block_count = feature_count // 128
    sign_table = (2 * sign_bits - 1).astype(jnp.float32).reshape(block_count, 128)
    hadamard_table = hadamard()
    shaped = stacked.reshape(3, bucket_rows, block_count, 128) * sign_table
    rotated = jnp.einsum("kubj,jc->kubc", shaped, hadamard_table, precision=lax.Precision.HIGHEST)
    scales = jnp.exp2(exponents.astype(jnp.float32))
    quantized = jnp.clip(rotated * scales[:, None, None, None], -127.0, 127.0).astype(jnp.bfloat16)
    flat_terms = lax.optimization_barrier(quantized).astype(jnp.float32).reshape(-1, 128)
    factors = jnp.exp2(-exponents.astype(jnp.float32)) / float(lax.axis_size("dp"))
    own_share = lax.psum_scatter(flat_terms, "dp", scatter_dimension=0, tiled=True).astype(
        jnp.bfloat16
    )
    gathered = lax.all_gather(own_share, "dp", axis=0, tiled=True)
    weight_grads = restore(gathered, factors, sign_table, hadamard_table)
    return (resid_grad, weight_grads)


def dispatch(n_dp, n_mp, *args):
    cols = args[0].shape[1]
    bucket = args[2].shape[1]
    whole = cols % 256 == 0 and bucket % 32 == 0 and cols >= 512
    if n_dp == 16 and n_mp == 2 and whole:
        return fused(n_dp, *args)
    return per_device(*args)


def solution(mesh):
    placed = (P("dp", "mp"), P("dp", "mp"), P(None, "mp", None), P(), P(), P())
    return jax.shard_map(
        functools.partial(dispatch, mesh.shape["dp"], mesh.shape["mp"]),
        mesh=mesh,
        in_specs=placed,
        out_specs=(P("dp", "mp"), P(None, "mp", None)),
        check_vma=False,
    )
```

```python
import functools
import math

import jax
import jax.numpy as jnp
from jax import lax
from jax.experimental import pallas as pl
from jax.experimental.pallas import tpu as pltpu
from jax.sharding import PartitionSpec as P

MESH = pl.DeviceIdType.MESH
F32 = jnp.float32
BF16 = jnp.bfloat16


def dot_nn(left, right):
    return lax.dot_general(left, right, (((1,), (0,)), ((), ())), preferred_element_type=F32)


def split_dot(left, right):
    high = left.astype(BF16)
    low = (left - high.astype(F32)).astype(BF16)
    return dot_nn(high, right) + dot_nn(low, right)


def signs_256():
    rows = lax.broadcasted_iota(jnp.int32, (256, 256), 0)
    cols = lax.broadcasted_iota(jnp.int32, (256, 256), 1)
    anded = jnp.bitwise_and(jnp.bitwise_and(rows, cols), 127)
    for shift in (4, 2, 1):
        anded = jnp.bitwise_xor(anded, jnp.right_shift(anded, shift))
    value = 1 - 2 * jnp.bitwise_and(anded, 1)
    same = jnp.right_shift(rows, 7) == jnp.right_shift(cols, 7)
    return jnp.where(same, value, 0).astype(F32).astype(BF16)


def to_column(row):
    return jnp.broadcast_to(row[0:1], (128, row.shape[1])).T


def pair(ref, first):
    return jnp.concatenate([ref[pl.ds(first, 1)], ref[pl.ds(first + 1, 1)]], axis=1)


def kernel(
    sizes,
    res_hbm,
    og_hbm,
    w_ref,
    gain_in,
    exp_ref,
    sign_in,
    rg_ref,
    out_ref,
    res_ref,
    og_ref,
    gain_ref,
    sign_ref,
    had,
    normed,
    column,
    wbuf,
    og_turned,
    normed_turned,
    sq_mine,
    sq_peer,
    part,
    part_out,
    part_in,
    *rest,
):
    n_dp, blocks, groups, chunks = sizes
    buffers = rest[:-3]
    local_sem, send_sem, recv_sem = rest[-3:]
    kinds = len(buffers) // len(chunks)
    cols = blocks * 128
    rows_w = 16 * groups
    split = groups // 2
    per_pair = 3 * split
    me = lax.axis_index("dp")
    side = lax.axis_index("mp")
    other = 1 - side
    core = me % 2
    y = (me // 2) % 2
    z = me // 4
    z_near = [z, z + 1 - 2 * (z % 2), (z + 2) % 4, 3 - z]
    first_block = side * blocks
    to_x = (me, other)
    to_core = (me + 1 - 2 * core, side)
    to_y = (me + 2 - 4 * y, side)
    to_z = [None] + [(zz * 4 + y * 2 + core, side) for zz in z_near[1:]]
    to_diagonal = [None] + [(target[0], other) for target in to_z[1:]]
    started = []

    def send(src, dst, target):
        index = len(started)
        copy = pltpu.make_async_remote_copy(
            src_ref=src,
            dst_ref=dst,
            send_sem=send_sem.at[index],
            recv_sem=recv_sem.at[index],
            device_id=target,
            device_id_type=MESH,
        )
        copy.start()
        started.append(copy)
        return copy

    barrier = pltpu.get_barrier_semaphore()
    partners = [to_x, to_core, to_y] + to_z[1:] + to_diagonal[1:]
    for target in partners:
        pl.semaphore_signal(barrier, inc=1, device_id=target, device_id_type=MESH)

    own_cols = pl.ds(pl.multiple_of(side * cols, 128), cols)
    get_res = pltpu.make_async_copy(res_hbm, res_ref, local_sem.at[0])
    get_res.start()
    get_og = pltpu.make_async_copy(og_hbm, og_ref, local_sem.at[1])
    get_og.start()
    get_w = pltpu.make_async_copy(w_ref.at[:, :, own_cols], wbuf.at[side], local_sem.at[2])
    get_w.start()
    had[...] = signs_256()
    gain_ref[...] = gain_in[...]
    sign_ref[...] = (2 * sign_in[...] - 1).astype(F32)
    core_rows = pl.ds(pl.multiple_of(core * (rows_w // 2), 16), rows_w // 2)
    pieces = 3
    cuts = [256 * (blocks // 2 * p // pieces) for p in range(pieces + 1)]

    def send_w(p):
        width = cuts[p + 1] - cuts[p]
        from_cols = pl.ds(pl.multiple_of(other * cols + cuts[p], 128), width)
        return send(
            w_ref.at[:, core_rows, from_cols],
            wbuf.at[side, :, core_rows, pl.ds(cuts[p], width)],
            to_x,
        )

    pl.semaphore_wait(barrier, len(partners))
    w_copies = [send_w(0)]
    get_res.wait()
    squares = jnp.zeros(column.shape[1:], F32)
    for j in range(blocks):
        wide = res_ref[:, 128 * j : 128 * j + 128].astype(F32)
        squares = squares + wide * wide
    sums = jnp.sum(squares.T, axis=0, keepdims=True)
    sq_mine[...] = jnp.broadcast_to(sums, sq_mine.shape)
    sq_copy = send(sq_mine, sq_peer, to_x)
    w_copies += [send_w(1), send_w(2)]
    shared = []

    def share_w(p):
        w_copies[p].wait_recv()
        landed = wbuf.at[other, :, core_rows, pl.ds(cuts[p], cuts[p + 1] - cuts[p])]
        shared.append(send(landed, landed, to_core))

    get_og.wait()
    for j in range(blocks):
        at = slice(128 * j, 128 * j + 128)
        og_turned[at] = og_ref[:, at].T
    get_w.wait()
    part[side, 2 * rows_w : 3 * rows_w] = dot_nn(wbuf[side, 2], og_turned[...])
    share_w(0)
    sq_copy.wait_recv()
    total_sq = sq_mine[...] + sq_peer[...]
    inverse = to_column(lax.rsqrt(total_sq / float(2 * cols) + 1e-06))
    column[0] = inverse
    for j in range(blocks):
        at = slice(128 * j, 128 * j + 128)
        unit = res_ref[:, at].astype(F32) * inverse
        scaled = (unit * gain_ref[pl.ds(first_block + j, 1)]).astype(BF16)
        normed[:, at] = scaled
        normed_turned[at] = scaled.T
    share_w(1)
    part[side, : 2 * rows_w] = dot_nn(
        wbuf[side, :2].reshape(2 * rows_w, cols), normed_turned[...]
    )
    part_out[side] = part[side].astype(BF16)
    own_part = send(part_out.at[side], part_in.at[side], to_x)

    share_w(2)
    pair_part = jnp.zeros((2 * rows_w, part.shape[2]), F32)
    down_part = jnp.zeros((rows_w, part.shape[2]), F32)
    for p in range(pieces):
        shared[p].wait_recv()
        at = slice(cuts[p], cuts[p + 1])
        weights = wbuf[other, :2, :, at].reshape(2 * rows_w, cuts[p + 1] - cuts[p])
        pair_part = pair_part + dot_nn(weights, normed_turned[at])
        down_part = down_part + dot_nn(wbuf[other, 2, :, at], og_turned[at])
    part[other, : 2 * rows_w] = pair_part
    part[other, 2 * rows_w : 3 * rows_w] = down_part
    part_out[other] = part[other].astype(BF16)
    peer_part = send(part_out.at[other], part_in.at[other], to_x)
    own_part.wait_recv()
    peer_part.wait_recv()

    pair_grads = []
    hiddens = []
    row_total = jnp.zeros((1, part.shape[2]), F32)
    for g in range(2):
        full = part[g] + part_in[g].astype(F32)
        gate_pre = full[:rows_w]
        up_proj = full[rows_w : 2 * rows_w]
        hidden_grad = full[2 * rows_w :]
        activated, slope = gelu_parts(gate_pre)
        hiddens.append((activated * up_proj).astype(BF16))
        gate_grad = (hidden_grad * up_proj * slope).astype(BF16)
        up_grad = (hidden_grad * activated).astype(BF16)
        pair_grads += [gate_grad, up_grad]
        row_total = row_total + jnp.sum(
            gate_grad.astype(F32) * gate_pre + up_grad.astype(F32) * up_proj,
            axis=0,
            keepdims=True,
        )
    pair_grad = jnp.concatenate(pair_grads, axis=0)
    hidden = jnp.concatenate(hiddens, axis=0)

    scales = [
        lax.shift_left(jnp.int32(1), exp_ref[k]).astype(F32) * (1.0 / math.sqrt(128.0))
        for k in range(3)
    ]
    order = [(0, 0), (0, 1), (1, 0), (1, 1), (0, 2), (1, 2)]

    class Chunk:
        pass

    lanes = []
    for q, (first_pair, pairs, window, starts) in enumerate(chunks):
        chunk = Chunk()
        lanes.append(chunk)
        chunk.first, chunk.pairs, chunk.window, chunk.starts = (
            first_pair,
            pairs,
            window,
            starts,
        )
        chunk.units = pairs * per_pair
        (
            chunk.terms,
            chunk.core_in,
            chunk.core_sum,
            chunk.y_in,
            chunk.y_sum,
            chunk.z_in,
            chunk.share,
            chunk.slots,
        ) = buffers[q * kinds : (q + 1) * kinds]

    def make_terms(chunk):
        table = had[...]
        for jj in range(chunk.first, chunk.first + chunk.pairs):
            at = slice(256 * jj, 256 * jj + 256)
            grads = jnp.concatenate(
                [dot_nn(pair_grad, normed[:, at]), dot_nn(hidden, og_ref[:, at])], axis=0
            )
            signed = grads * pair(sign_ref, first_block + 2 * jj)
            rotated = split_dot(signed, table)
            for index, (g, k) in enumerate(order):
                piece = rotated[index * rows_w : (index + 1) * rows_w] * scales[k]
                piece = jnp.clip(piece, -127.0, 127.0).astype(BF16)
                for b in range(2):
                    for i in range(groups):
                        unit_at = (jj - chunk.first) * per_pair + k * split + i % split
                        chunk.terms[i // split, b, g, unit_at] = piece[
                            16 * i : 16 * i + 16, 128 * b : 128 * b + 128
                        ]
        chunk.core_copy = send(chunk.terms.at[1 - core], chunk.core_in, to_core)

    def after_core(chunk):
        chunk.core_copy.wait_recv()
        chunk.core_sum[...] = (
            chunk.terms[core].astype(F32) + chunk.core_in[...].astype(F32)
        ).astype(BF16)
        chunk.y_copy = send(chunk.core_sum.at[1 - y], chunk.y_in, to_y)

    def after_y(chunk):
        chunk.y_copy.wait_recv()
        chunk.y_sum[...] = (
            chunk.core_sum[y].astype(F32) + chunk.y_in[...].astype(F32)
        ).astype(BF16)
        chunk.z_copies = []
        for o in (1, 2, 3):
            begin = chunk.units * z_near[o] // 4
            chunk.z_copies.append(
                send(chunk.y_sum.at[:, pl.ds(begin, chunk.window)], chunk.z_in.at[o - 1], to_z[o])
            )

    def after_z(chunk):
        window = chunk.window
        begin = chunk.units * z // 4
        summed = chunk.y_sum[:, pl.ds(begin, window)].astype(F32)
        for o in (1, 2, 3):
            chunk.z_copies[o - 1].wait_recv()
            summed = summed + chunk.z_in[o - 1].astype(F32)
        flat = summed.astype(BF16).reshape(2 * window * 16, 128)
        restored = dot_nn(flat, had[:128, :128]).reshape(2, window, 16, 128)
        for i in range(window):
            unit_at = begin + i
            block = 2 * (chunk.first + unit_at // per_pair) + y
            exponent = exp_ref[unit_at % per_pair // split]
            factor = lax.shift_left(jnp.int32(1), 30 - exponent).astype(F32) * (
                2.0**-30 / n_dp / math.sqrt(128.0)
            )
            turn = sign_ref[pl.ds(first_block + block, 1)] * factor
            for g in range(2):
                chunk.share[g, i] = (restored[g, i] * turn).astype(BF16)
        landing = chunk.slots.at[me, side]
        chunk.x_copy = send(chunk.share.at[other], landing, to_x)
        chunk.z_copies, chunk.diagonals = ([], [])
        for o in (1, 2, 3):
            chunk.diagonals.append(send(chunk.share.at[other], landing, to_diagonal[o]))
            chunk.z_copies.append(send(chunk.share.at[side], landing, to_z[o]))
        chunk.slots[me, side] = chunk.share[side]

    def forward(chunk, slot, targets):
        block = chunk.slots.at[slot]
        return [send(block, block, target) for target in targets]

    def after_x(chunk):
        chunk.x_copy.wait_recv()
        to_both = forward(chunk, me, [to_y, to_core])
        chunk.y_copies = to_both[:1]
        chunk.c_copies = to_both[1:]

    def gather_z(chunk):
        for o in (1, 2, 3):
            chunk.z_copies[o - 1].wait_recv()
            chunk.diagonals[o - 1].wait_recv()
            to_both = forward(chunk, z_near[o] * 4 + y * 2 + core, [to_y, to_core])
            chunk.y_copies.append(to_both[0])
            chunk.c_copies.append(to_both[1])

    def gather_y(chunk):
        for o in range(4):
            chunk.y_copies[o].wait_recv()
            chunk.c_copies += forward(
                chunk, z_near[o] * 4 + (1 - y) * 2 + core, [to_core]
            )

    def assemble(chunk):
        for copy in chunk.c_copies:
            copy.wait_recv()
        for slot in range(n_dp):
            zz, yy, cc = (slot // 4, slot // 2 % 2, slot % 2)
            for i in range(chunk.window):
                unit_at = chunk.starts[zz] + i
                if zz < 3 and unit_at >= chunk.starts[zz + 1]:
                    continue
                pair_at, rest_at = divmod(unit_at, per_pair)
                block = 2 * (chunk.first + pair_at) + yy
                k = rest_at // split
                top = 16 * (cc * split + rest_at % split)
                for fh in range(2):
                    lane = (fh * blocks + block) * 128
                    out_ref[k, top : top + 16, lane : lane + 128] = chunk.slots[slot, fh, i]

    def make_resid(first_pair, last_pair):
        row_mean = jnp.concatenate([column[1], column[1]], axis=1)
        inverse = jnp.concatenate([column[0], column[0]], axis=1)
        for jj in range(first_pair, last_pair):
            at = slice(256 * jj, 256 * jj + 256)
            normed_grad = jnp.zeros((res_ref.shape[0], 256), F32)
            for g in range(2):
                weights = wbuf[g, :2, :, at].reshape(2 * rows_w, 256)
                term = dot_nn(turned[:, 2 * rows_w * g : 2 * rows_w * (g + 1)], weights)
                normed_grad = normed_grad + term.astype(BF16).astype(F32)
            feature_grad = normed_grad * pair(gain_ref, first_block + 2 * jj)
            unit = res_ref[:, at].astype(F32) * inverse
            rg_ref[:, at] = (
                og_ref[:, at].astype(F32) + inverse * (feature_grad - unit * row_mean)
            ).astype(BF16)

    one, two = lanes
    all_pairs = blocks // 2
    make_terms(one)
    make_terms(two)
    after_core(one)
    column[1] = to_column(row_total / float(2 * cols))
    turned = pair_grad.astype(F32).T.astype(BF16)
    after_core(two)
    make_resid(0, all_pairs // 3)
    after_y(one)
    make_resid(all_pairs // 3, 2 * all_pairs // 3)
    after_y(two)
    after_z(one)
    make_resid(2 * all_pairs // 3, all_pairs)
    after_x(one)
    after_z(two)
    gather_z(one)
    after_x(two)
    gather_y(one)
    gather_z(two)
    gather_y(two)
    assemble(one)
    assemble(two)
    for copy in started:
        copy.wait_send()


COPIES = 9 + 2 * 24


def fused(n_dp, residual, out_grad, ffn_weights, norm_gain, exponents, sign_bits):
    tokens, cols = residual.shape
    bucket = ffn_weights.shape[1]
    blocks, groups = (cols // 128, bucket // 16)
    all_pairs = blocks // 2
    per_pair = 3 * groups // 2
    cut = all_pairs // 2
    vmem = pl.BlockSpec(memory_space=pltpu.VMEM)
    hbm = pl.BlockSpec(memory_space=pltpu.HBM)
    scratch = [
        pltpu.VMEM((tokens, cols), BF16),
        pltpu.VMEM((tokens, cols), BF16),
        pltpu.VMEM((2 * blocks, 128), F32),
        pltpu.VMEM((2 * blocks, 128), F32),
        pltpu.VMEM((256, 256), BF16),
        pltpu.VMEM((tokens, cols), BF16),
        pltpu.VMEM((2, tokens, 128), F32),
        pltpu.VMEM((2, 3, bucket, cols), BF16),
        pltpu.VMEM((cols, tokens), BF16),
        pltpu.VMEM((cols, tokens), BF16),
        pltpu.VMEM((8, tokens), F32),
        pltpu.VMEM((8, tokens), F32),
        pltpu.VMEM((2, 3 * bucket, tokens), F32),
        pltpu.VMEM((2, 3 * bucket, tokens), BF16),
        pltpu.VMEM((2, 3 * bucket, tokens), BF16),
    ]
    chunks = []
    for first, pairs in ((0, cut), (cut, all_pairs - cut)):
        units = pairs * per_pair
        window = -(-units // 4)
        chunks.append((first, pairs, window, [units * zz // 4 for zz in range(4)]))
        for lead in (
            (2, 2, 2, units),
            (2, 2, units),
            (2, 2, units),
            (2, units),
            (2, units),
            (3, 2, window),
            (2, window),
            (n_dp, 2, window),
        ):
            scratch.append(pltpu.VMEM(lead + (16, 128), BF16))
    scratch += [
        pltpu.SemaphoreType.DMA((3,)),
        pltpu.SemaphoreType.DMA((COPIES,)),
        pltpu.SemaphoreType.DMA((COPIES,)),
    ]
    return pl.pallas_call(
        functools.partial(kernel, (n_dp, blocks, groups, chunks)),
        out_shape=(
            pltpu.VMEM((tokens, cols), BF16),
            pltpu.VMEM(ffn_weights.shape, BF16),
        ),
        in_specs=[
            hbm,
            hbm,
            hbm,
            vmem,
            pl.BlockSpec(memory_space=pltpu.SMEM),
            vmem,
        ],
        out_specs=(vmem, vmem),
        scratch_shapes=scratch,
        compiler_params=pltpu.CompilerParams(
            collective_id=0, has_side_effects=True, vmem_limit_bytes=58 * 2**20
        ),
    )(
        residual,
        out_grad,
        ffn_weights,
        norm_gain.reshape(-1, 128),
        exponents,
        sign_bits.reshape(-1, 128),
    )


def hadamard():
    indices = jnp.arange(128, dtype=jnp.int32)
    anded = jnp.bitwise_and(indices[:, None], indices[None, :])
    parity = jnp.zeros((128, 128), jnp.int32)
    for offset in range(7):
        parity = parity + jnp.bitwise_and(jnp.right_shift(anded, offset), 1)
    return (1 - 2 * (parity % 2)).astype(jnp.float32) / math.sqrt(128.0)


def gelu_parts(values):
    tanh_input = 0.7978845608 * (values + 0.044715 * values * values * values)
    tanhed = jnp.tanh(tanh_input)
    forward = 0.5 * values * (1.0 + tanhed)
    gelu_slope = 0.5 * (1.0 + tanhed) + 0.5 * values * (1.0 - tanhed * tanhed) * 0.7978845608 * (
        1.0 + 3.0 * 0.044715 * values * values
    )
    return (forward, gelu_slope)


def restore(summed, factors, sign_table, hadamard_table):
    block_count = sign_table.shape[0]
    widened = lax.optimization_barrier(summed).astype(jnp.float32).reshape(3, -1, block_count, 128)
    scaled = widened * factors[:, None, None, None]
    restored = (
        jnp.einsum("kubj,jc->kubc", scaled, hadamard_table, precision=lax.Precision.HIGHEST)
        * sign_table
    )
    return restored.astype(jnp.bfloat16).reshape(3, -1, block_count * 128)


def per_device(residual, out_grad, ffn_weights, norm_gain, exponents, sign_bits):
    full_rows, grads_in = (
        lax.all_gather(residual, "mp", axis=1, tiled=True),
        lax.all_gather(out_grad, "mp", axis=1, tiled=True),
    )
    feature_count = full_rows.shape[1]
    col_count = residual.shape[1]
    col_start = lax.axis_index("mp") * col_count
    bucket_rows = ffn_weights.shape[1]
    rows_wide = full_rows.astype(jnp.float32)
    inverse = lax.rsqrt(jnp.mean(rows_wide * rows_wide, axis=1, keepdims=True) + 1e-06)
    unit_rows = rows_wide * inverse
    normed = (unit_rows * norm_gain).astype(jnp.bfloat16)
    pair_weights = ffn_weights[:2]
    gate_up = jnp.einsum("td,khd->tkh", normed, pair_weights, preferred_element_type=jnp.float32)
    gate_pre = gate_up[:, 0]
    up_proj = gate_up[:, 1]
    activated, gelu_slope = gelu_parts(gate_pre)
    hidden = (activated * up_proj).astype(jnp.bfloat16)
    hidden_grad = lax.dot_general(
        grads_in, ffn_weights[2], (((1,), (1,)), ((), ())), preferred_element_type=jnp.float32
    )
    gate_grad = (hidden_grad * up_proj * gelu_slope).astype(jnp.bfloat16)
    up_grad = (hidden_grad * activated).astype(jnp.bfloat16)
    pair_grad = jnp.stack([gate_grad, up_grad], axis=1)
    partial_value = jnp.einsum(
        "tkh,khd->td", pair_grad, pair_weights, preferred_element_type=jnp.float32
    )
    own_unit = lax.dynamic_slice_in_dim(unit_rows, col_start, col_count, 1)
    normed_grad = lax.psum(partial_value.astype(jnp.bfloat16), "mp").astype(jnp.float32)
    feature_grad = normed_grad * norm_gain
    row_mean = jnp.sum(feature_grad * unit_rows, axis=1, keepdims=True) / feature_count
    own_grad = lax.dynamic_slice_in_dim(feature_grad, col_start, col_count, 1)
    resid_grad = (out_grad.astype(jnp.float32) + inverse * (own_grad - own_unit * row_mean)).astype(
        jnp.bfloat16
    )
    pair_wgrad = jnp.einsum("tkh,td->khd", pair_grad, normed, preferred_element_type=jnp.float32)
    down_wgrad = lax.dot_general(
        hidden, grads_in, (((0,), (0,)), ((), ())), preferred_element_type=jnp.float32
    )
    stacked = jnp.concatenate([pair_wgrad, down_wgrad[None]], axis=0)
    block_count = feature_count // 128
    sign_table = (2 * sign_bits - 1).astype(jnp.float32).reshape(block_count, 128)
    hadamard_table = hadamard()
    shaped = stacked.reshape(3, bucket_rows, block_count, 128) * sign_table
    rotated = jnp.einsum("kubj,jc->kubc", shaped, hadamard_table, precision=lax.Precision.HIGHEST)
    scales = jnp.exp2(exponents.astype(jnp.float32))
    quantized = jnp.clip(rotated * scales[:, None, None, None], -127.0, 127.0).astype(jnp.bfloat16)
    flat_terms = lax.optimization_barrier(quantized).astype(jnp.float32).reshape(-1, 128)
    factors = jnp.exp2(-exponents.astype(jnp.float32)) / float(lax.axis_size("dp"))
    own_share = lax.psum_scatter(flat_terms, "dp", scatter_dimension=0, tiled=True).astype(
        jnp.bfloat16
    )
    gathered = lax.all_gather(own_share, "dp", axis=0, tiled=True)
    weight_grads = restore(gathered, factors, sign_table, hadamard_table)
    return (resid_grad, weight_grads)


def dispatch(n_dp, n_mp, *args):
    cols = args[0].shape[1]
    bucket = args[2].shape[1]
    whole = cols % 256 == 0 and bucket % 32 == 0 and cols >= 512
    if n_dp == 16 and n_mp == 2 and whole:
        return fused(n_dp, *args)
    return per_device(*args)


def solution(mesh):
    placed = (P("dp", "mp"), P("dp", "mp"), P(None, "mp", None), P(), P(), P())
    return jax.shard_map(
        functools.partial(dispatch, mesh.shape["dp"], mesh.shape["mp"]),
        mesh=mesh,
        in_specs=placed,
        out_specs=(P("dp", "mp"), P(None, "mp", None)),
        check_vma=False,
    )
```

```python
import functools
import math

import jax
import jax.numpy as jnp
from jax import lax
from jax.experimental import pallas as pl
from jax.experimental.pallas import tpu as pltpu
from jax.sharding import PartitionSpec as P

MESH = pl.DeviceIdType.MESH
F32 = jnp.float32
BF16 = jnp.bfloat16


def dot_nn(left, right):
    return lax.dot_general(left, right, (((1,), (0,)), ((), ())), preferred_element_type=F32)


def split_dot(left, right):
    high = left.astype(BF16)
    low = (left - high.astype(F32)).astype(BF16)
    both = dot_nn(jnp.concatenate([high, low], axis=0), right)
    return both[: left.shape[0]] + both[left.shape[0] :]


def signs_256():
    rows = lax.broadcasted_iota(jnp.int32, (256, 256), 0)
    cols = lax.broadcasted_iota(jnp.int32, (256, 256), 1)
    anded = jnp.bitwise_and(jnp.bitwise_and(rows, cols), 127)
    for shift in (4, 2, 1):
        anded = jnp.bitwise_xor(anded, jnp.right_shift(anded, shift))
    value = 1 - 2 * jnp.bitwise_and(anded, 1)
    same = jnp.right_shift(rows, 7) == jnp.right_shift(cols, 7)
    return jnp.where(same, value, 0).astype(F32).astype(BF16)


def to_column(row):
    return jnp.broadcast_to(row[0:1], (128, row.shape[1])).T


def pair(ref, first):
    return jnp.concatenate([ref[pl.ds(first, 1)], ref[pl.ds(first + 1, 1)]], axis=1)


def kernel(
    sizes,
    res_hbm,
    og_hbm,
    w_ref,
    gain_in,
    exp_ref,
    sign_in,
    rg_ref,
    out_ref,
    res_ref,
    og_ref,
    gain_ref,
    sign_ref,
    had,
    normed,
    column,
    wbuf,
    og_turned,
    normed_turned,
    sq_mine,
    sq_peer,
    part,
    part_out,
    part_in,
    *rest,
):
    n_dp, blocks, groups, chunks = sizes
    buffers = rest[:-3]
    local_sem, send_sem, recv_sem = rest[-3:]
    kinds = len(buffers) // len(chunks)
    cols = blocks * 128
    rows_w = 16 * groups
    split = groups // 2
    per_pair = 3 * split
    me = lax.axis_index("dp")
    side = lax.axis_index("mp")
    other = 1 - side
    core = me % 2
    y = (me // 2) % 2
    z = me // 4
    z_near = [z, z + 1 - 2 * (z % 2), (z + 2) % 4, 3 - z]
    first_block = side * blocks
    to_x = (me, other)
    to_core = (me + 1 - 2 * core, side)
    to_y = (me + 2 - 4 * y, side)
    to_z = [None] + [(zz * 4 + y * 2 + core, side) for zz in z_near[1:]]
    to_diagonal = [None] + [(target[0], other) for target in to_z[1:]]
    started = []

    def send(src, dst, target):
        index = len(started)
        copy = pltpu.make_async_remote_copy(
            src_ref=src,
            dst_ref=dst,
            send_sem=send_sem.at[index],
            recv_sem=recv_sem.at[index],
            device_id=target,
            device_id_type=MESH,
        )
        copy.start()
        started.append(copy)
        return copy

    barrier = pltpu.get_barrier_semaphore()
    partners = [to_x, to_core, to_y] + to_z[1:] + to_diagonal[1:]
    for target in partners:
        pl.semaphore_signal(barrier, inc=1, device_id=target, device_id_type=MESH)

    own_cols = pl.ds(pl.multiple_of(side * cols, 128), cols)
    get_res = pltpu.make_async_copy(res_hbm, res_ref, local_sem.at[0])
    get_res.start()
    get_og = pltpu.make_async_copy(og_hbm, og_ref, local_sem.at[1])
    get_og.start()
    get_w = pltpu.make_async_copy(w_ref.at[:, :, own_cols], wbuf.at[side], local_sem.at[2])
    get_w.start()
    had[...] = signs_256()
    gain_ref[...] = gain_in[...]
    sign_ref[...] = (2 * sign_in[...] - 1).astype(F32)
    core_rows = pl.ds(pl.multiple_of(core * (rows_w // 2), 16), rows_w // 2)
    pieces = 3
    cuts = [256 * (blocks // 2 * p // pieces) for p in range(pieces + 1)]

    def send_w(p):
        width = cuts[p + 1] - cuts[p]
        from_cols = pl.ds(pl.multiple_of(other * cols + cuts[p], 128), width)
        return send(
            w_ref.at[:, core_rows, from_cols],
            wbuf.at[side, :, core_rows, pl.ds(cuts[p], width)],
            to_x,
        )

    pl.semaphore_wait(barrier, len(partners))
    w_copies = [send_w(0)]
    get_res.wait()
    squares = jnp.zeros(column.shape[1:], F32)
    for j in range(blocks):
        wide = res_ref[:, 128 * j : 128 * j + 128].astype(F32)
        squares = squares + wide * wide
    sums = jnp.sum(squares.T, axis=0, keepdims=True)
    sq_mine[...] = jnp.broadcast_to(sums, sq_mine.shape)
    sq_copy = send(sq_mine, sq_peer, to_x)
    w_copies += [send_w(1), send_w(2)]
    shared = []

    def share_w(p):
        w_copies[p].wait_recv()
        landed = wbuf.at[other, :, core_rows, pl.ds(cuts[p], cuts[p + 1] - cuts[p])]
        shared.append(send(landed, landed, to_core))

    get_og.wait()
    for j in range(blocks):
        at = slice(128 * j, 128 * j + 128)
        og_turned[at] = og_ref[:, at].T
    get_w.wait()
    part[side, 2 * rows_w : 3 * rows_w] = dot_nn(wbuf[side, 2], og_turned[...])
    share_w(0)
    sq_copy.wait_recv()
    total_sq = sq_mine[...] + sq_peer[...]
    inverse = to_column(lax.rsqrt(total_sq / float(2 * cols) + 1e-06))
    column[0] = inverse
    for j in range(blocks):
        at = slice(128 * j, 128 * j + 128)
        unit = res_ref[:, at].astype(F32) * inverse
        scaled = (unit * gain_ref[pl.ds(first_block + j, 1)]).astype(BF16)
        normed[:, at] = scaled
        normed_turned[at] = scaled.T
    share_w(1)
    part[side, : 2 * rows_w] = dot_nn(
        wbuf[side, :2].reshape(2 * rows_w, cols), normed_turned[...]
    )
    part_out[side] = part[side].astype(BF16)
    own_part = send(part_out.at[side], part_in.at[side], to_x)

    share_w(2)
    pair_part = jnp.zeros((2 * rows_w, part.shape[2]), F32)
    down_part = jnp.zeros((rows_w, part.shape[2]), F32)
    for p in range(pieces):
        shared[p].wait_recv()
        at = slice(cuts[p], cuts[p + 1])
        weights = wbuf[other, :2, :, at].reshape(2 * rows_w, cuts[p + 1] - cuts[p])
        pair_part = pair_part + dot_nn(weights, normed_turned[at])
        down_part = down_part + dot_nn(wbuf[other, 2, :, at], og_turned[at])
    part[other, : 2 * rows_w] = pair_part
    part[other, 2 * rows_w : 3 * rows_w] = down_part
    part_out[other] = part[other].astype(BF16)
    peer_part = send(part_out.at[other], part_in.at[other], to_x)
    own_part.wait_recv()
    peer_part.wait_recv()

    pair_grads = []
    hiddens = []
    row_total = jnp.zeros((1, part.shape[2]), F32)
    for g in range(2):
        full = part[g] + part_in[g].astype(F32)
        gate_pre = full[:rows_w]
        up_proj = full[rows_w : 2 * rows_w]
        hidden_grad = full[2 * rows_w :]
        activated, slope = gelu_parts(gate_pre)
        hiddens.append((activated * up_proj).astype(BF16))
        gate_grad = (hidden_grad * up_proj * slope).astype(BF16)
        up_grad = (hidden_grad * activated).astype(BF16)
        pair_grads += [gate_grad, up_grad]
        row_total = row_total + jnp.sum(
            gate_grad.astype(F32) * gate_pre + up_grad.astype(F32) * up_proj,
            axis=0,
            keepdims=True,
        )
    pair_grad = jnp.concatenate(pair_grads, axis=0)
    hidden = jnp.concatenate(hiddens, axis=0)

    scales = [
        lax.shift_left(jnp.int32(1), exp_ref[k]).astype(F32) * (1.0 / math.sqrt(128.0))
        for k in range(3)
    ]
    order = [(0, 0), (0, 1), (1, 0), (1, 1), (0, 2), (1, 2)]

    class Chunk:
        pass

    lanes = []
    for q, (first_pair, pairs, window, starts) in enumerate(chunks):
        chunk = Chunk()
        lanes.append(chunk)
        chunk.first, chunk.pairs, chunk.window, chunk.starts = (
            first_pair,
            pairs,
            window,
            starts,
        )
        chunk.units = pairs * per_pair
        (
            chunk.terms,
            chunk.core_in,
            chunk.core_sum,
            chunk.y_in,
            chunk.y_sum,
            chunk.z_in,
            chunk.share,
            chunk.slots,
        ) = buffers[q * kinds : (q + 1) * kinds]

    def make_terms(chunk):
        table = had[...]
        for jj in range(chunk.first, chunk.first + chunk.pairs):
            at = slice(256 * jj, 256 * jj + 256)
            grads = jnp.concatenate(
                [dot_nn(pair_grad, normed[:, at]), dot_nn(hidden, og_ref[:, at])], axis=0
            )
            signed = grads * pair(sign_ref, first_block + 2 * jj)
            rotated = split_dot(signed, table)
            for index, (g, k) in enumerate(order):
                piece = rotated[index * rows_w : (index + 1) * rows_w] * scales[k]
                piece = jnp.clip(piece, -127.0, 127.0).astype(BF16)
                for b in range(2):
                    for i in range(groups):
                        unit_at = (jj - chunk.first) * per_pair + k * split + i % split
                        chunk.terms[i // split, b, g, unit_at] = piece[
                            16 * i : 16 * i + 16, 128 * b : 128 * b + 128
                        ]
        chunk.core_copy = send(chunk.terms.at[1 - core], chunk.core_in, to_core)

    def after_core(chunk):
        chunk.core_copy.wait_recv()
        chunk.core_sum[...] = (
            chunk.terms[core].astype(F32) + chunk.core_in[...].astype(F32)
        ).astype(BF16)
        chunk.y_copy = send(chunk.core_sum.at[1 - y], chunk.y_in, to_y)

    def after_y(chunk):
        chunk.y_copy.wait_recv()
        chunk.y_sum[...] = (
            chunk.core_sum[y].astype(F32) + chunk.y_in[...].astype(F32)
        ).astype(BF16)
        chunk.z_copies = []
        for o in (1, 2, 3):
            begin = chunk.units * z_near[o] // 4
            chunk.z_copies.append(
                send(chunk.y_sum.at[:, pl.ds(begin, chunk.window)], chunk.z_in.at[o - 1], to_z[o])
            )

    def after_z(chunk):
        window = chunk.window
        begin = chunk.units * z // 4
        summed = chunk.y_sum[:, pl.ds(begin, window)].astype(F32)
        for o in (1, 2, 3):
            chunk.z_copies[o - 1].wait_recv()
            summed = summed + chunk.z_in[o - 1].astype(F32)
        flat = summed.astype(BF16).reshape(2 * window * 16, 128)
        restored = dot_nn(flat, had[:128, :128]).reshape(2, window, 16, 128)
        for i in range(window):
            unit_at = begin + i
            block = 2 * (chunk.first + unit_at // per_pair) + y
            exponent = exp_ref[unit_at % per_pair // split]
            factor = lax.shift_left(jnp.int32(1), 30 - exponent).astype(F32) * (
                2.0**-30 / n_dp / math.sqrt(128.0)
            )
            turn = sign_ref[pl.ds(first_block + block, 1)] * factor
            for g in range(2):
                chunk.share[g, i] = (restored[g, i] * turn).astype(BF16)
        landing = chunk.slots.at[me, side]
        chunk.x_copy = send(chunk.share.at[other], landing, to_x)
        chunk.z_copies, chunk.diagonals = ([], [])
        for o in (1, 2, 3):
            chunk.diagonals.append(send(chunk.share.at[other], landing, to_diagonal[o]))
            chunk.z_copies.append(send(chunk.share.at[side], landing, to_z[o]))
        chunk.slots[me, side] = chunk.share[side]

    def forward(chunk, slot, targets):
        block = chunk.slots.at[slot]
        return [send(block, block, target) for target in targets]

    def after_x(chunk):
        chunk.x_copy.wait_recv()
        to_both = forward(chunk, me, [to_y, to_core])
        chunk.y_copies = to_both[:1]
        chunk.c_copies = to_both[1:]

    def gather_z(chunk):
        for o in (1, 2, 3):
            chunk.z_copies[o - 1].wait_recv()
            chunk.diagonals[o - 1].wait_recv()
            to_both = forward(chunk, z_near[o] * 4 + y * 2 + core, [to_y, to_core])
            chunk.y_copies.append(to_both[0])
            chunk.c_copies.append(to_both[1])

    def gather_y(chunk):
        for o in range(4):
            chunk.y_copies[o].wait_recv()
            chunk.c_copies += forward(
                chunk, z_near[o] * 4 + (1 - y) * 2 + core, [to_core]
            )

    def assemble(chunk):
        for copy in chunk.c_copies:
            copy.wait_recv()
        for slot in range(n_dp):
            zz, yy, cc = (slot // 4, slot // 2 % 2, slot % 2)
            for i in range(chunk.window):
                unit_at = chunk.starts[zz] + i
                if zz < 3 and unit_at >= chunk.starts[zz + 1]:
                    continue
                pair_at, rest_at = divmod(unit_at, per_pair)
                block = 2 * (chunk.first + pair_at) + yy
                k = rest_at // split
                top = 16 * (cc * split + rest_at % split)
                for fh in range(2):
                    lane = (fh * blocks + block) * 128
                    out_ref[k, top : top + 16, lane : lane + 128] = chunk.slots[slot, fh, i]

    def make_resid(first_pair, last_pair):
        row_mean = jnp.concatenate([column[1], column[1]], axis=1)
        inverse = jnp.concatenate([column[0], column[0]], axis=1)
        for jj in range(first_pair, last_pair):
            at = slice(256 * jj, 256 * jj + 256)
            normed_grad = jnp.zeros((res_ref.shape[0], 256), F32)
            for g in range(2):
                weights = wbuf[g, :2, :, at].reshape(2 * rows_w, 256)
                term = dot_nn(turned[:, 2 * rows_w * g : 2 * rows_w * (g + 1)], weights)
                normed_grad = normed_grad + term.astype(BF16).astype(F32)
            feature_grad = normed_grad * pair(gain_ref, first_block + 2 * jj)
            unit = res_ref[:, at].astype(F32) * inverse
            rg_ref[:, at] = (
                og_ref[:, at].astype(F32) + inverse * (feature_grad - unit * row_mean)
            ).astype(BF16)

    one, two, three = lanes
    all_pairs = blocks // 2
    make_terms(one)
    make_terms(two)
    after_core(one)
    make_terms(three)
    after_core(two)
    column[1] = to_column(row_total / float(2 * cols))
    turned = pair_grad.astype(F32).T.astype(BF16)
    after_y(one)
    after_core(three)
    make_resid(0, all_pairs // 3)
    after_y(two)
    after_z(one)
    make_resid(all_pairs // 3, 2 * all_pairs // 3)
    after_y(three)
    after_x(one)
    make_resid(2 * all_pairs // 3, all_pairs)
    after_z(two)
    gather_z(one)
    after_x(two)
    gather_y(one)
    after_z(three)
    gather_z(two)
    after_x(three)
    gather_y(two)
    gather_z(three)
    assemble(one)
    gather_y(three)
    assemble(two)
    assemble(three)
    for copy in started:
        copy.wait_send()


COPIES = 9 + 3 * 24


def fused(n_dp, residual, out_grad, ffn_weights, norm_gain, exponents, sign_bits):
    tokens, cols = residual.shape
    bucket = ffn_weights.shape[1]
    blocks, groups = (cols // 128, bucket // 16)
    all_pairs = blocks // 2
    per_pair = 3 * groups // 2
    half = all_pairs // 2
    lead_pairs = all_pairs - 2 * half or 1
    vmem = pl.BlockSpec(memory_space=pltpu.VMEM)
    hbm = pl.BlockSpec(memory_space=pltpu.HBM)
    scratch = [
        pltpu.VMEM((tokens, cols), BF16),
        pltpu.VMEM((tokens, cols), BF16),
        pltpu.VMEM((2 * blocks, 128), F32),
        pltpu.VMEM((2 * blocks, 128), F32),
        pltpu.VMEM((256, 256), BF16),
        pltpu.VMEM((tokens, cols), BF16),
        pltpu.VMEM((2, tokens, 128), F32),
        pltpu.VMEM((2, 3, bucket, cols), BF16),
        pltpu.VMEM((cols, tokens), BF16),
        pltpu.VMEM((cols, tokens), BF16),
        pltpu.VMEM((8, tokens), F32),
        pltpu.VMEM((8, tokens), F32),
        pltpu.VMEM((2, 3 * bucket, tokens), F32),
        pltpu.VMEM((2, 3 * bucket, tokens), BF16),
        pltpu.VMEM((2, 3 * bucket, tokens), BF16),
    ]
    chunks = []
    for first, pairs in (
        (0, lead_pairs),
        (lead_pairs, half),
        (lead_pairs + half, all_pairs - lead_pairs - half),
    ):
        units = pairs * per_pair
        window = -(-units // 4)
        chunks.append((first, pairs, window, [units * zz // 4 for zz in range(4)]))
        for lead in (
            (2, 2, 2, units),
            (2, 2, units),
            (2, 2, units),
            (2, units),
            (2, units),
            (3, 2, window),
            (2, window),
            (n_dp, 2, window),
        ):
            scratch.append(pltpu.VMEM(lead + (16, 128), BF16))
    scratch += [
        pltpu.SemaphoreType.DMA((3,)),
        pltpu.SemaphoreType.DMA((COPIES,)),
        pltpu.SemaphoreType.DMA((COPIES,)),
    ]
    return pl.pallas_call(
        functools.partial(kernel, (n_dp, blocks, groups, chunks)),
        out_shape=(
            pltpu.VMEM((tokens, cols), BF16),
            pltpu.VMEM(ffn_weights.shape, BF16),
        ),
        in_specs=[
            hbm,
            hbm,
            hbm,
            vmem,
            pl.BlockSpec(memory_space=pltpu.SMEM),
            vmem,
        ],
        out_specs=(vmem, vmem),
        scratch_shapes=scratch,
        compiler_params=pltpu.CompilerParams(
            collective_id=0, has_side_effects=True, vmem_limit_bytes=58 * 2**20
        ),
    )(
        residual,
        out_grad,
        ffn_weights,
        norm_gain.reshape(-1, 128),
        exponents,
        sign_bits.reshape(-1, 128),
    )


def hadamard():
    indices = jnp.arange(128, dtype=jnp.int32)
    anded = jnp.bitwise_and(indices[:, None], indices[None, :])
    parity = jnp.zeros((128, 128), jnp.int32)
    for offset in range(7):
        parity = parity + jnp.bitwise_and(jnp.right_shift(anded, offset), 1)
    return (1 - 2 * (parity % 2)).astype(jnp.float32) / math.sqrt(128.0)


def gelu_parts(values):
    tanh_input = 0.7978845608 * (values + 0.044715 * values * values * values)
    tanhed = jnp.tanh(tanh_input)
    forward = 0.5 * values * (1.0 + tanhed)
    gelu_slope = 0.5 * (1.0 + tanhed) + 0.5 * values * (1.0 - tanhed * tanhed) * 0.7978845608 * (
        1.0 + 3.0 * 0.044715 * values * values
    )
    return (forward, gelu_slope)


def restore(summed, factors, sign_table, hadamard_table):
    block_count = sign_table.shape[0]
    widened = lax.optimization_barrier(summed).astype(jnp.float32).reshape(3, -1, block_count, 128)
    scaled = widened * factors[:, None, None, None]
    restored = (
        jnp.einsum("kubj,jc->kubc", scaled, hadamard_table, precision=lax.Precision.HIGHEST)
        * sign_table
    )
    return restored.astype(jnp.bfloat16).reshape(3, -1, block_count * 128)


def per_device(residual, out_grad, ffn_weights, norm_gain, exponents, sign_bits):
    full_rows, grads_in = (
        lax.all_gather(residual, "mp", axis=1, tiled=True),
        lax.all_gather(out_grad, "mp", axis=1, tiled=True),
    )
    feature_count = full_rows.shape[1]
    col_count = residual.shape[1]
    col_start = lax.axis_index("mp") * col_count
    bucket_rows = ffn_weights.shape[1]
    rows_wide = full_rows.astype(jnp.float32)
    inverse = lax.rsqrt(jnp.mean(rows_wide * rows_wide, axis=1, keepdims=True) + 1e-06)
    unit_rows = rows_wide * inverse
    normed = (unit_rows * norm_gain).astype(jnp.bfloat16)
    pair_weights = ffn_weights[:2]
    gate_up = jnp.einsum("td,khd->tkh", normed, pair_weights, preferred_element_type=jnp.float32)
    gate_pre = gate_up[:, 0]
    up_proj = gate_up[:, 1]
    activated, gelu_slope = gelu_parts(gate_pre)
    hidden = (activated * up_proj).astype(jnp.bfloat16)
    hidden_grad = lax.dot_general(
        grads_in, ffn_weights[2], (((1,), (1,)), ((), ())), preferred_element_type=jnp.float32
    )
    gate_grad = (hidden_grad * up_proj * gelu_slope).astype(jnp.bfloat16)
    up_grad = (hidden_grad * activated).astype(jnp.bfloat16)
    pair_grad = jnp.stack([gate_grad, up_grad], axis=1)
    partial_value = jnp.einsum(
        "tkh,khd->td", pair_grad, pair_weights, preferred_element_type=jnp.float32
    )
    own_unit = lax.dynamic_slice_in_dim(unit_rows, col_start, col_count, 1)
    normed_grad = lax.psum(partial_value.astype(jnp.bfloat16), "mp").astype(jnp.float32)
    feature_grad = normed_grad * norm_gain
    row_mean = jnp.sum(feature_grad * unit_rows, axis=1, keepdims=True) / feature_count
    own_grad = lax.dynamic_slice_in_dim(feature_grad, col_start, col_count, 1)
    resid_grad = (out_grad.astype(jnp.float32) + inverse * (own_grad - own_unit * row_mean)).astype(
        jnp.bfloat16
    )
    pair_wgrad = jnp.einsum("tkh,td->khd", pair_grad, normed, preferred_element_type=jnp.float32)
    down_wgrad = lax.dot_general(
        hidden, grads_in, (((0,), (0,)), ((), ())), preferred_element_type=jnp.float32
    )
    stacked = jnp.concatenate([pair_wgrad, down_wgrad[None]], axis=0)
    block_count = feature_count // 128
    sign_table = (2 * sign_bits - 1).astype(jnp.float32).reshape(block_count, 128)
    hadamard_table = hadamard()
    shaped = stacked.reshape(3, bucket_rows, block_count, 128) * sign_table
    rotated = jnp.einsum("kubj,jc->kubc", shaped, hadamard_table, precision=lax.Precision.HIGHEST)
    scales = jnp.exp2(exponents.astype(jnp.float32))
    quantized = jnp.clip(rotated * scales[:, None, None, None], -127.0, 127.0).astype(jnp.bfloat16)
    flat_terms = lax.optimization_barrier(quantized).astype(jnp.float32).reshape(-1, 128)
    factors = jnp.exp2(-exponents.astype(jnp.float32)) / float(lax.axis_size("dp"))
    own_share = lax.psum_scatter(flat_terms, "dp", scatter_dimension=0, tiled=True).astype(
        jnp.bfloat16
    )
    gathered = lax.all_gather(own_share, "dp", axis=0, tiled=True)
    weight_grads = restore(gathered, factors, sign_table, hadamard_table)
    return (resid_grad, weight_grads)


def dispatch(n_dp, n_mp, *args):
    cols = args[0].shape[1]
    bucket = args[2].shape[1]
    whole = cols % 256 == 0 and bucket % 32 == 0 and cols >= 768
    if n_dp == 16 and n_mp == 2 and whole:
        return fused(n_dp, *args)
    return per_device(*args)


def solution(mesh):
    placed = (P("dp", "mp"), P("dp", "mp"), P(None, "mp", None), P(), P(), P())
    return jax.shard_map(
        functools.partial(dispatch, mesh.shape["dp"], mesh.shape["mp"]),
        mesh=mesh,
        in_specs=placed,
        out_specs=(P("dp", "mp"), P(None, "mp", None)),
        check_vma=False,
    )
```

```python
import functools
import math

import jax
import jax.numpy as jnp
from jax import lax
from jax.experimental import pallas as pl
from jax.experimental.pallas import tpu as pltpu
from jax.sharding import PartitionSpec as P

MESH = pl.DeviceIdType.MESH
F32 = jnp.float32
BF16 = jnp.bfloat16


def dot_nn(left, right):
    return lax.dot_general(left, right, (((1,), (0,)), ((), ())), preferred_element_type=F32)


def split_dot(left, right):
    high = left.astype(BF16)
    low = (left - high.astype(F32)).astype(BF16)
    return dot_nn(high, right) + dot_nn(low, right)


def signs_256():
    rows = lax.broadcasted_iota(jnp.int32, (256, 256), 0)
    cols = lax.broadcasted_iota(jnp.int32, (256, 256), 1)
    anded = jnp.bitwise_and(jnp.bitwise_and(rows, cols), 127)
    for shift in (4, 2, 1):
        anded = jnp.bitwise_xor(anded, jnp.right_shift(anded, shift))
    value = 1 - 2 * jnp.bitwise_and(anded, 1)
    same = jnp.right_shift(rows, 7) == jnp.right_shift(cols, 7)
    return jnp.where(same, value, 0).astype(F32).astype(BF16)


def to_column(row):
    return jnp.broadcast_to(row[0:1], (128, row.shape[1])).T


def pair(ref, first):
    return jnp.concatenate([ref[pl.ds(first, 1)], ref[pl.ds(first + 1, 1)]], axis=1)


def kernel(
    sizes,
    res_hbm,
    og_hbm,
    w_ref,
    gain_in,
    exp_ref,
    sign_in,
    rg_ref,
    out_ref,
    res_ref,
    og_ref,
    gain_ref,
    sign_ref,
    had,
    normed,
    column,
    wbuf,
    og_turned,
    normed_turned,
    sq_mine,
    sq_peer,
    part,
    part_out,
    part_in,
    *rest,
):
    n_dp, blocks, groups, chunks = sizes
    buffers = rest[:-3]
    local_sem, send_sem, recv_sem = rest[-3:]
    kinds = len(buffers) // len(chunks)
    cols = blocks * 128
    rows_w = 16 * groups
    split = groups // 2
    per_pair = 3 * split
    me = lax.axis_index("dp")
    side = lax.axis_index("mp")
    other = 1 - side
    core = me % 2
    y = (me // 2) % 2
    z = me // 4
    z_near = [z, z + 1 - 2 * (z % 2), (z + 2) % 4, 3 - z]
    first_block = side * blocks
    to_x = (me, other)
    to_core = (me + 1 - 2 * core, side)
    to_y = (me + 2 - 4 * y, side)
    to_z = [None] + [(zz * 4 + y * 2 + core, side) for zz in z_near[1:]]
    to_diagonal = [None] + [(target[0], other) for target in to_z[1:]]
    started = []

    def send(src, dst, target):
        index = len(started)
        copy = pltpu.make_async_remote_copy(
            src_ref=src,
            dst_ref=dst,
            send_sem=send_sem.at[index],
            recv_sem=recv_sem.at[index],
            device_id=target,
            device_id_type=MESH,
        )
        copy.start()
        started.append(copy)
        return copy

    barrier = pltpu.get_barrier_semaphore()
    partners = [to_x, to_core, to_y] + to_z[1:] + to_diagonal[1:]
    for target in partners:
        pl.semaphore_signal(barrier, inc=1, device_id=target, device_id_type=MESH)

    own_cols = pl.ds(pl.multiple_of(side * cols, 128), cols)
    get_res = pltpu.make_async_copy(res_hbm, res_ref, local_sem.at[0])
    get_res.start()
    get_og = pltpu.make_async_copy(og_hbm, og_ref, local_sem.at[1])
    get_og.start()
    get_w = pltpu.make_async_copy(w_ref.at[:, :, own_cols], wbuf.at[side], local_sem.at[2])
    get_w.start()
    had[...] = signs_256()
    gain_ref[...] = gain_in[...]
    sign_ref[...] = (2 * sign_in[...] - 1).astype(F32)
    core_rows = pl.ds(pl.multiple_of(core * (rows_w // 2), 16), rows_w // 2)
    pieces = 3
    cuts = [256 * (blocks // 2 * p // pieces) for p in range(pieces + 1)]

    def send_w(p):
        width = cuts[p + 1] - cuts[p]
        from_cols = pl.ds(pl.multiple_of(other * cols + cuts[p], 128), width)
        return send(
            w_ref.at[:, core_rows, from_cols],
            wbuf.at[side, :, core_rows, pl.ds(cuts[p], width)],
            to_x,
        )

    pl.semaphore_wait(barrier, len(partners))
    w_copies = [send_w(0)]
    get_res.wait()
    squares = jnp.zeros(column.shape[1:], F32)
    for j in range(blocks):
        wide = res_ref[:, 128 * j : 128 * j + 128].astype(F32)
        squares = squares + wide * wide
    sums = jnp.sum(squares.T, axis=0, keepdims=True)
    sq_mine[...] = jnp.broadcast_to(sums, sq_mine.shape)
    sq_copy = send(sq_mine, sq_peer, to_x)
    w_copies += [send_w(1), send_w(2)]
    shared = []

    def share_w(p):
        w_copies[p].wait_recv()
        landed = wbuf.at[other, :, core_rows, pl.ds(cuts[p], cuts[p + 1] - cuts[p])]
        shared.append(send(landed, landed, to_core))

    get_og.wait()
    for j in range(blocks):
        at = slice(128 * j, 128 * j + 128)
        og_turned[at] = og_ref[:, at].T
    get_w.wait()
    part[side, 2 * rows_w : 3 * rows_w] = dot_nn(wbuf[side, 2], og_turned[...])
    share_w(0)
    sq_copy.wait_recv()
    total_sq = sq_mine[...] + sq_peer[...]
    inverse = to_column(lax.rsqrt(total_sq / float(2 * cols) + 1e-06))
    column[0] = inverse
    for j in range(blocks):
        at = slice(128 * j, 128 * j + 128)
        unit = res_ref[:, at].astype(F32) * inverse
        scaled = (unit * gain_ref[pl.ds(first_block + j, 1)]).astype(BF16)
        normed[:, at] = scaled
        normed_turned[at] = scaled.T
    share_w(1)
    part[side, : 2 * rows_w] = dot_nn(
        wbuf[side, :2].reshape(2 * rows_w, cols), normed_turned[...]
    )
    part_out[side] = part[side].astype(BF16)
    own_part = send(part_out.at[side], part_in.at[side], to_x)

    share_w(2)
    pair_part = jnp.zeros((2 * rows_w, part.shape[2]), F32)
    down_part = jnp.zeros((rows_w, part.shape[2]), F32)
    for p in range(pieces):
        shared[p].wait_recv()
        at = slice(cuts[p], cuts[p + 1])
        weights = wbuf[other, :2, :, at].reshape(2 * rows_w, cuts[p + 1] - cuts[p])
        pair_part = pair_part + dot_nn(weights, normed_turned[at])
        down_part = down_part + dot_nn(wbuf[other, 2, :, at], og_turned[at])
    part[other, : 2 * rows_w] = pair_part
    part[other, 2 * rows_w : 3 * rows_w] = down_part
    part_out[other] = part[other].astype(BF16)
    peer_part = send(part_out.at[other], part_in.at[other], to_x)
    own_part.wait_recv()
    peer_part.wait_recv()

    pair_grads = []
    hiddens = []
    row_total = jnp.zeros((1, part.shape[2]), F32)
    for g in range(2):
        full = part[g] + part_in[g].astype(F32)
        gate_pre = full[:rows_w]
        up_proj = full[rows_w : 2 * rows_w]
        hidden_grad = full[2 * rows_w :]
        activated, slope = gelu_parts(gate_pre)
        hiddens.append((activated * up_proj).astype(BF16))
        gate_grad = (hidden_grad * up_proj * slope).astype(BF16)
        up_grad = (hidden_grad * activated).astype(BF16)
        pair_grads += [gate_grad, up_grad]
        row_total = row_total + jnp.sum(
            gate_grad.astype(F32) * gate_pre + up_grad.astype(F32) * up_proj,
            axis=0,
            keepdims=True,
        )
    pair_grad = jnp.concatenate(pair_grads, axis=0)
    hidden = jnp.concatenate(hiddens, axis=0)

    scales = [
        lax.shift_left(jnp.int32(1), exp_ref[k]).astype(F32) * (1.0 / math.sqrt(128.0))
        for k in range(3)
    ]
    order = [(0, 0), (0, 1), (1, 0), (1, 1), (0, 2), (1, 2)]

    class Chunk:
        pass

    lanes = []
    for q, (first_pair, pairs, window, starts) in enumerate(chunks):
        chunk = Chunk()
        lanes.append(chunk)
        chunk.first, chunk.pairs, chunk.window, chunk.starts = (
            first_pair,
            pairs,
            window,
            starts,
        )
        chunk.units = pairs * per_pair
        (
            chunk.terms,
            chunk.core_in,
            chunk.core_sum,
            chunk.y_in,
            chunk.y_sum,
            chunk.z_in,
            chunk.share,
            chunk.slots,
        ) = buffers[q * kinds : (q + 1) * kinds]

    def make_terms(chunk):
        table = had[...]
        for jj in range(chunk.first, chunk.first + chunk.pairs):
            at = slice(256 * jj, 256 * jj + 256)
            grads = jnp.concatenate(
                [dot_nn(pair_grad, normed[:, at]), dot_nn(hidden, og_ref[:, at])], axis=0
            )
            signed = grads * pair(sign_ref, first_block + 2 * jj)
            rotated = split_dot(signed, table)
            for index, (g, k) in enumerate(order):
                piece = rotated[index * rows_w : (index + 1) * rows_w] * scales[k]
                piece = jnp.clip(piece, -127.0, 127.0).astype(BF16)
                for b in range(2):
                    for i in range(groups):
                        unit_at = (jj - chunk.first) * per_pair + k * split + i % split
                        chunk.terms[i // split, b, g, unit_at] = piece[
                            16 * i : 16 * i + 16, 128 * b : 128 * b + 128
                        ]
        chunk.core_copy = send(chunk.terms.at[1 - core], chunk.core_in, to_core)

    def after_core(chunk):
        chunk.core_copy.wait_recv()
        chunk.core_sum[...] = (
            chunk.terms[core].astype(F32) + chunk.core_in[...].astype(F32)
        ).astype(BF16)
        chunk.y_copy = send(chunk.core_sum.at[1 - y], chunk.y_in, to_y)

    def after_y(chunk):
        chunk.y_copy.wait_recv()
        chunk.y_sum[...] = (
            chunk.core_sum[y].astype(F32) + chunk.y_in[...].astype(F32)
        ).astype(BF16)
        chunk.z_copies = []
        for o in (1, 2, 3):
            begin = chunk.units * z_near[o] // 4
            chunk.z_copies.append(
                send(chunk.y_sum.at[:, pl.ds(begin, chunk.window)], chunk.z_in.at[o - 1], to_z[o])
            )

    def after_z(chunk):
        window = chunk.window
        begin = chunk.units * z // 4
        summed = chunk.y_sum[:, pl.ds(begin, window)].astype(F32)
        for o in (1, 2, 3):
            chunk.z_copies[o - 1].wait_recv()
            summed = summed + chunk.z_in[o - 1].astype(F32)
        flat = summed.astype(BF16).reshape(2 * window * 16, 128)
        restored = dot_nn(flat, had[:128, :128]).reshape(2, window, 16, 128)
        for i in range(window):
            unit_at = begin + i
            block = 2 * (chunk.first + unit_at // per_pair) + y
            exponent = exp_ref[unit_at % per_pair // split]
            factor = lax.shift_left(jnp.int32(1), 30 - exponent).astype(F32) * (
                2.0**-30 / n_dp / math.sqrt(128.0)
            )
            turn = sign_ref[pl.ds(first_block + block, 1)] * factor
            for g in range(2):
                chunk.share[g, i] = (restored[g, i] * turn).astype(BF16)
        landing = chunk.slots.at[me, side]
        chunk.x_copy = send(chunk.share.at[other], landing, to_x)
        chunk.z_copies, chunk.diagonals = ([], [])
        for o in (1, 2, 3):
            chunk.diagonals.append(send(chunk.share.at[other], landing, to_diagonal[o]))
            chunk.z_copies.append(send(chunk.share.at[side], landing, to_z[o]))
        chunk.slots[me, side] = chunk.share[side]

    def forward(chunk, slot, targets):
        block = chunk.slots.at[slot]
        return [send(block, block, target) for target in targets]

    def after_x(chunk):
        chunk.x_copy.wait_recv()
        to_both = forward(chunk, me, [to_y, to_core])
        chunk.y_copies = to_both[:1]
        chunk.c_copies = to_both[1:]

    def gather_z(chunk):
        for o in (1, 2, 3):
            chunk.z_copies[o - 1].wait_recv()
            chunk.diagonals[o - 1].wait_recv()
            to_both = forward(chunk, z_near[o] * 4 + y * 2 + core, [to_y, to_core])
            chunk.y_copies.append(to_both[0])
            chunk.c_copies.append(to_both[1])

    def gather_y(chunk):
        for o in range(4):
            chunk.y_copies[o].wait_recv()
            chunk.c_copies += forward(
                chunk, z_near[o] * 4 + (1 - y) * 2 + core, [to_core]
            )

    def assemble(chunk):
        for copy in chunk.c_copies:
            copy.wait_recv()
        for slot in range(n_dp):
            zz, yy, cc = (slot // 4, slot // 2 % 2, slot % 2)
            for i in range(chunk.window):
                unit_at = chunk.starts[zz] + i
                if zz < 3 and unit_at >= chunk.starts[zz + 1]:
                    continue
                pair_at, rest_at = divmod(unit_at, per_pair)
                block = 2 * (chunk.first + pair_at) + yy
                k = rest_at // split
                top = 16 * (cc * split + rest_at % split)
                for fh in range(2):
                    lane = (fh * blocks + block) * 128
                    out_ref[k, top : top + 16, lane : lane + 128] = chunk.slots[slot, fh, i]

    def make_resid(first_pair, last_pair):
        row_mean = jnp.concatenate([column[1], column[1]], axis=1)
        inverse = jnp.concatenate([column[0], column[0]], axis=1)
        for jj in range(first_pair, last_pair):
            at = slice(256 * jj, 256 * jj + 256)
            normed_grad = jnp.zeros((res_ref.shape[0], 256), F32)
            for g in range(2):
                weights = wbuf[g, :2, :, at].reshape(2 * rows_w, 256)
                term = dot_nn(turned[:, 2 * rows_w * g : 2 * rows_w * (g + 1)], weights)
                normed_grad = normed_grad + term.astype(BF16).astype(F32)
            feature_grad = normed_grad * pair(gain_ref, first_block + 2 * jj)
            unit = res_ref[:, at].astype(F32) * inverse
            rg_ref[:, at] = (
                og_ref[:, at].astype(F32) + inverse * (feature_grad - unit * row_mean)
            ).astype(BF16)

    one, two = lanes
    all_pairs = blocks // 2
    make_terms(one)
    make_terms(two)
    after_core(one)
    column[1] = to_column(row_total / float(2 * cols))
    turned = pair_grad.astype(F32).T.astype(BF16)
    after_core(two)
    make_resid(0, all_pairs // 3)
    after_y(one)
    make_resid(all_pairs // 3, 2 * all_pairs // 3)
    after_y(two)
    after_z(one)
    make_resid(2 * all_pairs // 3, all_pairs)
    after_x(one)
    after_z(two)
    gather_z(one)
    after_x(two)
    gather_y(one)
    gather_z(two)
    gather_y(two)
    assemble(one)
    assemble(two)
    for copy in started:
        copy.wait_send()


COPIES = 9 + 2 * 24


def fused(n_dp, residual, out_grad, ffn_weights, norm_gain, exponents, sign_bits):
    tokens, cols = residual.shape
    bucket = ffn_weights.shape[1]
    blocks, groups = (cols // 128, bucket // 16)
    all_pairs = blocks // 2
    per_pair = 3 * groups // 2
    cut = all_pairs - all_pairs // 2
    vmem = pl.BlockSpec(memory_space=pltpu.VMEM)
    hbm = pl.BlockSpec(memory_space=pltpu.HBM)
    scratch = [
        pltpu.VMEM((tokens, cols), BF16),
        pltpu.VMEM((tokens, cols), BF16),
        pltpu.VMEM((2 * blocks, 128), F32),
        pltpu.VMEM((2 * blocks, 128), F32),
        pltpu.VMEM((256, 256), BF16),
        pltpu.VMEM((tokens, cols), BF16),
        pltpu.VMEM((2, tokens, 128), F32),
        pltpu.VMEM((2, 3, bucket, cols), BF16),
        pltpu.VMEM((cols, tokens), BF16),
        pltpu.VMEM((cols, tokens), BF16),
        pltpu.VMEM((8, tokens), F32),
        pltpu.VMEM((8, tokens), F32),
        pltpu.VMEM((2, 3 * bucket, tokens), F32),
        pltpu.VMEM((2, 3 * bucket, tokens), BF16),
        pltpu.VMEM((2, 3 * bucket, tokens), BF16),
    ]
    chunks = []
    for first, pairs in ((0, cut), (cut, all_pairs - cut)):
        units = pairs * per_pair
        window = -(-units // 4)
        chunks.append((first, pairs, window, [units * zz // 4 for zz in range(4)]))
        for lead in (
            (2, 2, 2, units),
            (2, 2, units),
            (2, 2, units),
            (2, units),
            (2, units),
            (3, 2, window),
            (2, window),
            (n_dp, 2, window),
        ):
            scratch.append(pltpu.VMEM(lead + (16, 128), BF16))
    scratch += [
        pltpu.SemaphoreType.DMA((3,)),
        pltpu.SemaphoreType.DMA((COPIES,)),
        pltpu.SemaphoreType.DMA((COPIES,)),
    ]
    return pl.pallas_call(
        functools.partial(kernel, (n_dp, blocks, groups, chunks)),
        out_shape=(
            pltpu.VMEM((tokens, cols), BF16),
            pltpu.VMEM(ffn_weights.shape, BF16),
        ),
        in_specs=[
            hbm,
            hbm,
            hbm,
            vmem,
            pl.BlockSpec(memory_space=pltpu.SMEM),
            vmem,
        ],
        out_specs=(vmem, vmem),
        scratch_shapes=scratch,
        compiler_params=pltpu.CompilerParams(
            collective_id=0, has_side_effects=True, vmem_limit_bytes=58 * 2**20
        ),
    )(
        residual,
        out_grad,
        ffn_weights,
        norm_gain.reshape(-1, 128),
        exponents,
        sign_bits.reshape(-1, 128),
    )


def hadamard():
    indices = jnp.arange(128, dtype=jnp.int32)
    anded = jnp.bitwise_and(indices[:, None], indices[None, :])
    parity = jnp.zeros((128, 128), jnp.int32)
    for offset in range(7):
        parity = parity + jnp.bitwise_and(jnp.right_shift(anded, offset), 1)
    return (1 - 2 * (parity % 2)).astype(jnp.float32) / math.sqrt(128.0)


def gelu_parts(values):
    tanh_input = 0.7978845608 * (values + 0.044715 * values * values * values)
    tanhed = jnp.tanh(tanh_input)
    forward = 0.5 * values * (1.0 + tanhed)
    gelu_slope = 0.5 * (1.0 + tanhed) + 0.5 * values * (1.0 - tanhed * tanhed) * 0.7978845608 * (
        1.0 + 3.0 * 0.044715 * values * values
    )
    return (forward, gelu_slope)


def restore(summed, factors, sign_table, hadamard_table):
    block_count = sign_table.shape[0]
    widened = lax.optimization_barrier(summed).astype(jnp.float32).reshape(3, -1, block_count, 128)
    scaled = widened * factors[:, None, None, None]
    restored = (
        jnp.einsum("kubj,jc->kubc", scaled, hadamard_table, precision=lax.Precision.HIGHEST)
        * sign_table
    )
    return restored.astype(jnp.bfloat16).reshape(3, -1, block_count * 128)


def per_device(residual, out_grad, ffn_weights, norm_gain, exponents, sign_bits):
    full_rows, grads_in = (
        lax.all_gather(residual, "mp", axis=1, tiled=True),
        lax.all_gather(out_grad, "mp", axis=1, tiled=True),
    )
    feature_count = full_rows.shape[1]
    col_count = residual.shape[1]
    col_start = lax.axis_index("mp") * col_count
    bucket_rows = ffn_weights.shape[1]
    rows_wide = full_rows.astype(jnp.float32)
    inverse = lax.rsqrt(jnp.mean(rows_wide * rows_wide, axis=1, keepdims=True) + 1e-06)
    unit_rows = rows_wide * inverse
    normed = (unit_rows * norm_gain).astype(jnp.bfloat16)
    pair_weights = ffn_weights[:2]
    gate_up = jnp.einsum("td,khd->tkh", normed, pair_weights, preferred_element_type=jnp.float32)
    gate_pre = gate_up[:, 0]
    up_proj = gate_up[:, 1]
    activated, gelu_slope = gelu_parts(gate_pre)
    hidden = (activated * up_proj).astype(jnp.bfloat16)
    hidden_grad = lax.dot_general(
        grads_in, ffn_weights[2], (((1,), (1,)), ((), ())), preferred_element_type=jnp.float32
    )
    gate_grad = (hidden_grad * up_proj * gelu_slope).astype(jnp.bfloat16)
    up_grad = (hidden_grad * activated).astype(jnp.bfloat16)
    pair_grad = jnp.stack([gate_grad, up_grad], axis=1)
    partial_value = jnp.einsum(
        "tkh,khd->td", pair_grad, pair_weights, preferred_element_type=jnp.float32
    )
    own_unit = lax.dynamic_slice_in_dim(unit_rows, col_start, col_count, 1)
    normed_grad = lax.psum(partial_value.astype(jnp.bfloat16), "mp").astype(jnp.float32)
    feature_grad = normed_grad * norm_gain
    row_mean = jnp.sum(feature_grad * unit_rows, axis=1, keepdims=True) / feature_count
    own_grad = lax.dynamic_slice_in_dim(feature_grad, col_start, col_count, 1)
    resid_grad = (out_grad.astype(jnp.float32) + inverse * (own_grad - own_unit * row_mean)).astype(
        jnp.bfloat16
    )
    pair_wgrad = jnp.einsum("tkh,td->khd", pair_grad, normed, preferred_element_type=jnp.float32)
    down_wgrad = lax.dot_general(
        hidden, grads_in, (((0,), (0,)), ((), ())), preferred_element_type=jnp.float32
    )
    stacked = jnp.concatenate([pair_wgrad, down_wgrad[None]], axis=0)
    block_count = feature_count // 128
    sign_table = (2 * sign_bits - 1).astype(jnp.float32).reshape(block_count, 128)
    hadamard_table = hadamard()
    shaped = stacked.reshape(3, bucket_rows, block_count, 128) * sign_table
    rotated = jnp.einsum("kubj,jc->kubc", shaped, hadamard_table, precision=lax.Precision.HIGHEST)
    scales = jnp.exp2(exponents.astype(jnp.float32))
    quantized = jnp.clip(rotated * scales[:, None, None, None], -127.0, 127.0).astype(jnp.bfloat16)
    flat_terms = lax.optimization_barrier(quantized).astype(jnp.float32).reshape(-1, 128)
    factors = jnp.exp2(-exponents.astype(jnp.float32)) / float(lax.axis_size("dp"))
    own_share = lax.psum_scatter(flat_terms, "dp", scatter_dimension=0, tiled=True).astype(
        jnp.bfloat16
    )
    gathered = lax.all_gather(own_share, "dp", axis=0, tiled=True)
    weight_grads = restore(gathered, factors, sign_table, hadamard_table)
    return (resid_grad, weight_grads)


def dispatch(n_dp, n_mp, *args):
    cols = args[0].shape[1]
    bucket = args[2].shape[1]
    whole = cols % 256 == 0 and bucket % 32 == 0 and cols >= 512
    if n_dp == 16 and n_mp == 2 and whole:
        return fused(n_dp, *args)
    return per_device(*args)


def solution(mesh):
    placed = (P("dp", "mp"), P("dp", "mp"), P(None, "mp", None), P(), P(), P())
    return jax.shard_map(
        functools.partial(dispatch, mesh.shape["dp"], mesh.shape["mp"]),
        mesh=mesh,
        in_specs=placed,
        out_specs=(P("dp", "mp"), P(None, "mp", None)),
        check_vma=False,
    )
```
